256 devices in a mesh: tm: 32 (over y, z_hi, core), space: 8 (over z_lo, x).
Axes of the slice: x: 4, y: 4, z: 8 (z_hi: 4, z_lo: 2; z = z_hi * 2 + z_lo), core: 2. Of those that a mesh axis runs over, the one named last changes fastest.
Arguments:
- prev_starts: float32 [32, 4, 4, 64, 128], P('tm', None, None, 'space'), may hold values from -6 to 6
- plan: int32 [32, 2], P('tm'), may hold values from 0 to 7
- cell_type: int32 [4, 64, 128], P(None, 'space'), may hold values from 0 to 2
- coarse_matrix: float32 [4, 4, 4, 64, 128], P(None, None, None, 'space'), may hold values from -0.02 to 0.94, as said below
- rate_values: float32 [8], replicated, may hold values from 0.5 to 3
- enc_weight: float32 [4, 128], replicated, may hold values from -3 to 3
- type_table: float32 [3, 128], replicated, may hold values from -3 to 3
- force_vector: float32 [128], replicated, may hold values from -6 to 6
- norm_gain: float32 [6, 128], replicated, may hold values from 0.5 to 1.5
- self_weight: bfloat16 [6, 128, 128], replicated, may hold values from -0.5 to 0.5
- neigh_weight: bfloat16 [6, 128, 128], replicated, may hold values from -0.21875 to 0.21875
- out_weight: bfloat16 [6, 128, 128], replicated, may hold values from -0.5 to 0.5
- layer_bias: float32 [6, 128], replicated, may hold values from -3 to 3
- dec_gain: float32 [128], replicated, may hold values from 0.5 to 1.5
- dec_weight: bfloat16 [4, 128], replicated, may hold values from -0.25 to 0.25
Outputs:
- corrected_ends: float32 [32, 4, 4, 64, 128], P('tm', None, None, 'space')
The draws below stay inside these ranges and needn't reach their ends.
Inputs may be any that keep to these rules, and one draw needn't show every extreme that they name: `coarse_matrix`: diagonal entries are positive and in each cell the absolute entries of a row sum to at most 1.
All inputs are finite; a program needn't handle non-finite values.
Results may differ from the reference program's by a relative error of at most 0.0065.
Values may be sent and summed in bfloat16 or wider, within the bound.
No kernel may reach another device: no remote copies, remote signals or barrier semaphores. Data moves between devices by JAX's collectives and lax.ppermute only.
A program may use at most 64 MiB of HBM per device.

```python
import math
import jax
import jax.numpy as jnp
from jax import lax

HID = 128
CHAN = 4
NZ = 4
TYPES = 3
RATES = 8
LAYERS = 6
STEPS = 2
NY = 128
NX = 64
WINDOWS = 32


def draw_coarse_matrix(key, part):
    key = jax.random.fold_in(key, 7)
    first_key, second_key = jax.random.split(key)
    shape = (CHAN, CHAN, NZ, NX, NY)
    decay_rate = jnp.exp(jax.random.uniform(first_key, shape, jnp.float32, math.log(0.001), math.log(0.3)))
    coupling = jax.random.uniform(second_key, shape, jnp.float32, -0.02, 0.02)
    diagonal = 0.94 * jnp.exp(-decay_rate)
    identity = jnp.eye(CHAN, dtype=jnp.float32)[:, :, None, None, None]
    return identity * diagonal + (1.0 - identity) * coupling


def with_ends(drawn, key, smallest, largest):
    spot = [jax.random.randint(jax.random.fold_in(key, axis), (), 0, length) for axis, length in enumerate(drawn.shape)]
    widest = drawn.shape.index(max(drawn.shape))
    neighbour = spot[:widest] + [(spot[widest] + 1) % drawn.shape[widest]] + spot[widest + 1:]
    return drawn.at[tuple(spot)].set(smallest).at[tuple(neighbour)].set(largest)


def shard_levels(rng, shape, cuts, low, high):
    gain, own = 1.0, jax.random.fold_in(rng, 6)
    for axis_at, parts in cuts:
        draws = jnp.exp(jax.random.uniform(jax.random.fold_in(own, axis_at), (parts,), jnp.float32, low / len(cuts), high / len(cuts)))
        gain = gain * jnp.repeat(draws, shape[axis_at] // parts).reshape([-1 if axis == axis_at else 1 for axis in range(len(shape))])
    return gain


def noise(stream_key, dims, spread, reach, cuts=(), held_as=jnp.bfloat16):
    array = jax.random.normal(stream_key, dims, jnp.float32) * spread
    if len(cuts) > 0:
        array = shard_levels(stream_key, dims, cuts, -0.22, 0.18) * array
    return jnp.clip(array, min=-reach, max=reach).astype(held_as)


def setup_inputs(seed: int = 0) -> dict:
    streams_of = jax.random.split(jax.random.key(seed), 16)
    prev_starts = noise(streams_of[0], (WINDOWS, CHAN, NZ, NX, NY), 1.0, 6.0, ((0, 32), (3, 8)), jnp.float32)
    plan = with_ends(jax.random.randint(streams_of[1], (WINDOWS, STEPS), 0, RATES), jax.random.fold_in(streams_of[1], 1), 0, RATES - 1).astype(jnp.int32)
    cell_type = with_ends(jax.random.randint(streams_of[2], (NZ, NX, NY), 0, TYPES), jax.random.fold_in(streams_of[2], 1), 0, TYPES - 1).astype(jnp.int32)
    coarse_matrix = draw_coarse_matrix(jax.random.fold_in(streams_of[15], 71), 0)
    rate_values = jnp.clip(jnp.exp(jax.random.uniform(streams_of[4], (RATES,), jnp.float32, math.log(0.5), math.log(3.0))), 0.5, 3.0)
    enc_weight = noise(streams_of[5], (CHAN, HID), CHAN ** -0.5, 3.0, (), jnp.float32)
    type_table = noise(streams_of[6], (TYPES, HID), 0.5, 3.0, (), jnp.float32)
    force_vector = noise(streams_of[7], (HID,), 1.0, 6.0, (), jnp.float32)
    norm_gain = jnp.clip(1.0 + 0.1 * jax.random.normal(streams_of[8], (LAYERS, HID), jnp.float32), 0.5, 1.5)
    self_weight = noise(streams_of[9], (LAYERS, HID, HID), HID ** -0.5, 0.5)
    neigh_weight = noise(streams_of[10], (LAYERS, HID, HID), (6 * HID) ** -0.5, 0.21875)
    out_weight = noise(streams_of[11], (LAYERS, HID, HID), HID ** -0.5, 0.5)
    layer_bias = noise(streams_of[12], (LAYERS, HID), 0.5, 3.0, (), jnp.float32)
    dec_gain = jnp.clip(1.0 + 0.1 * jax.random.normal(streams_of[13], (HID,), jnp.float32), 0.5, 1.5)
    dec_weight = noise(streams_of[14], (CHAN, HID), (4 * HID) ** -0.5, 0.25)
    return dict(prev_starts=prev_starts, plan=plan, cell_type=cell_type, coarse_matrix=coarse_matrix, rate_values=rate_values, enc_weight=enc_weight, type_table=type_table, force_vector=force_vector, norm_gain=norm_gain, self_weight=self_weight, neigh_weight=neigh_weight, out_weight=out_weight, layer_bias=layer_bias, dec_gain=dec_gain, dec_weight=dec_weight)


EPS = 1e-05

def normed(hidden, gain_row):
    widened = hidden.astype(jnp.float32)
    row_mean = lax.optimization_barrier(jnp.mean(widened, axis=-1, keepdims=True))
    row_var = lax.optimization_barrier(jnp.mean(jnp.square(widened - row_mean), axis=-1, keepdims=True))
    return (widened - row_mean) * lax.rsqrt(row_var + EPS) * gain_row

def neighbours(padded):
    centre = padded[:, 1:-1]
    summed = padded[:, :-2].astype(jnp.float32) + padded[:, 2:].astype(jnp.float32)
    along_y = jnp.pad(centre, ((0, 0), (0, 0), (1, 1), (0, 0)))
    summed = summed + along_y[:, :, :-2].astype(jnp.float32) + along_y[:, :, 2:].astype(jnp.float32)
    along_z = jnp.pad(centre, ((1, 1), (0, 0), (0, 0), (0, 0)))
    summed = summed + along_z[:-2].astype(jnp.float32) + along_z[2:].astype(jnp.float32)
    return summed.astype(jnp.bfloat16)

def advance(hidden_mid, padded, self_w, neigh_w, out_w, bias_row):
    neigh_sum = neighbours(padded)
    centre = padded[:, 1:-1]
    preact = jnp.dot(centre, self_w, preferred_element_type=jnp.float32)
    preact = preact + jnp.dot(neigh_sum, neigh_w, preferred_element_type=jnp.float32) + bias_row
    message = jax.nn.silu(preact).astype(jnp.bfloat16)
    return (hidden_mid.astype(jnp.float32) + jnp.dot(message, out_w, preferred_element_type=jnp.float32)).astype(jnp.bfloat16)

def encode(window_state, cell_type, rate_value, enc_weight, type_table, force_vector):
    hidden = window_state[0][..., None] * enc_weight[0]
    for channel in range(1, CHAN):
        hidden = hidden + window_state[channel][..., None] * enc_weight[channel]
    for kind_index in range(TYPES):
        hidden = hidden + (cell_type == kind_index).astype(jnp.float32)[..., None] * type_table[kind_index]
    well_sign = (cell_type == 1).astype(jnp.float32) - (cell_type == 2).astype(jnp.float32)
    hidden = hidden + (well_sign * rate_value)[..., None] * force_vector
    return hidden.astype(jnp.bfloat16)

def lookup_rate(sched_row, step_index, rate_values):
    picks = jnp.arange(RATES, dtype=jnp.int32) == sched_row[step_index]
    return jnp.sum(jnp.where(picks, rate_values, 0.0))

def decode(hidden, dec_gain, dec_weight):
    decoded = normed(hidden, dec_gain).astype(jnp.bfloat16)
    return jnp.einsum('ch,zxyh->czxy', dec_weight.astype(jnp.float32), decoded.astype(jnp.float32))

def matvec(matrix, vector):
    return lax.optimization_barrier(jnp.sum(matrix * vector[None], axis=1))

def propagate(window_state, sched_row, cell_type, rate_values, enc_weight, type_table, force_vector, norm_gain, self_weight, neigh_weight, out_weight, layer_bias, dec_gain, dec_weight):
    for step_index in range(STEPS):
        rate_value = lookup_rate(sched_row, step_index, rate_values)
        hidden = encode(window_state, cell_type, rate_value, enc_weight, type_table, force_vector)
        for layer_index in range(LAYERS):
            normalized = normed(hidden, norm_gain[layer_index]).astype(jnp.bfloat16)
            padded = jnp.pad(normalized, ((0, 0), (1, 1), (0, 0), (0, 0)))
            hidden = advance(hidden, padded, self_weight[layer_index], neigh_weight[layer_index], out_weight[layer_index], layer_bias[layer_index])
        window_state = window_state + decode(hidden, dec_gain, dec_weight)
    return window_state

def reference(prev_starts, plan, cell_type, coarse_matrix, rate_values, enc_weight, type_table, force_vector, norm_gain, self_weight, neigh_weight, out_weight, layer_bias, dec_gain, dec_weight):

    def one_window(window_pair):
        return propagate(window_pair[0], window_pair[1], cell_type, rate_values, enc_weight, type_table, force_vector, norm_gain, self_weight, neigh_weight, out_weight, layer_bias, dec_gain, dec_weight)
    fine_ends = lax.map(one_window, (prev_starts, plan))

    def correct(current, window_pair):
        updated = window_pair[0] + matvec(coarse_matrix, current - window_pair[1])
        return (updated, updated)
    _, corrected_ends = lax.scan(correct, prev_starts[0], (fine_ends, prev_starts))
    return corrected_ends
```

```python
import functools

import jax
import jax.numpy as jnp
import numpy as np
from jax import lax
from jax.experimental import pallas as pl
from jax.experimental.pallas import tpu as pltpu
from jax.sharding import PartitionSpec as P

HID = 128
CHAN = 4
NZ = 4
TYPES = 3
RATES = 8
LAYERS = 6
STEPS = 2
NY = 128

EPS = 1e-05

GROUPS, GROUP = 8, 16
PADDED = (GROUPS + 2) * GROUP
BLOCK = 8
FRAME = 3 * BLOCK
FEATURES = 3 * CHAN + 2 * TYPES

F32, BF16 = jnp.float32, jnp.bfloat16

_row = np.arange(NY)
TO_GROUPS = np.zeros((NY, NY), np.float32)
TO_GROUPS[_row, (_row % GROUP) * GROUPS + _row // GROUP] = 1.0


def dot(a, b, **kw):
    return jnp.dot(a, b, preferred_element_type=F32, **kw)


def dot_nt(a, b):
    return lax.dot_general(a, b, (((1,), (1,)), ((), ())), preferred_element_type=F32)


def halves(value):
    high = value.astype(BF16)
    return high, (value - high.astype(F32)).astype(BF16)


def fine_step(
    where_ref, own_ref, first_ref, second_ref, kind_ref, kind_first_ref, kind_second_ref,
    enc_ref, in_ref, out_ref, bias_ref, gain_ref, dec_ref, order_ref, back_ref,
    state_ref, send_ref,
    hidden_ref, norm_ref, message_ref,
):
    position = where_ref[0]
    last = where_ref[1]
    odd = position % 2 == 1
    at_left = position == 0
    at_right = position == last

    def store_normalized(layer, x, z, hidden):
        slot = layer % 2
        square = jnp.sum(hidden * hidden, axis=-1, keepdims=True) * (1.0 / HID)
        normal = hidden * lax.rsqrt(square + EPS) * gain_ref[layer]
        norm_ref[slot, x, z, GROUP : GROUP + NY, :] = normal.astype(BF16)
        line = lax.broadcasted_iota(jnp.int32, (GROUP, HID), 0)
        before = pltpu.roll(normal[NY - GROUP :], 1, 0)
        before = jnp.where(line == 0, 0.0, before)
        norm_ref[slot, x, z, :GROUP, :] = before.astype(BF16)
        after = pltpu.roll(normal[:GROUP], GROUP - 1, 0)
        after = jnp.where(line == GROUP - 1, 0.0, after)
        norm_ref[slot, x, z, GROUP + NY :, :] = after.astype(BF16)

    @pl.when(at_left)
    def _():
        norm_ref[:, BLOCK - 1] = jnp.zeros((2, NZ, PADDED, HID), BF16)

    @pl.when(at_right)
    def _():
        norm_ref[:, 2 * BLOCK] = jnp.zeros((2, NZ, PADDED, HID), BF16)

    def encode(block, states, kinds, z):
        rows = []
        highs = [state.astype(BF16).astype(F32) for state in states]
        rows.extend(highs)
        rows.extend(state - high for state, high in zip(states, highs))
        rows.extend(highs)
        marks = [(kinds == kind).astype(F32) for kind in range(TYPES)]
        rows.extend(marks)
        rows.extend(marks)
        table = jnp.concatenate(rows, axis=0).astype(BF16)
        turned = dot_nt(order_ref[...], table).astype(BF16)
        for x in range(BLOCK):
            hidden = dot(turned, enc_ref[:, x * HID : (x + 1) * HID])
            hidden_ref[block * BLOCK + x, z] = hidden
            store_normalized(0, block * BLOCK + x, z, hidden)

    for z in range(NZ):
        encode(
            1,
            [own_ref[c, z] for c in range(CHAN)],
            kind_ref[z],
            z,
        )

    def neighbour(block, take_first):
        for z in range(NZ):
            states = []
            for c in range(CHAN):
                at = pl.ds((c * NZ + z) * BLOCK, BLOCK)
                states.append(jnp.where(take_first, first_ref[at, :], second_ref[at, :]))
            at = pl.ds(z * BLOCK, BLOCK)
            kinds = jnp.where(take_first, kind_first_ref[at, :], kind_second_ref[at, :])
            encode(block, states, kinds, z)

    @pl.when(jnp.logical_not(at_left))
    def _():
        neighbour(0, odd)

    @pl.when(jnp.logical_not(at_right))
    def _():
        neighbour(2, jnp.logical_not(odd))

    def rows_of(layer):
        reach = LAYERS - 1 - layer
        low = jnp.where(at_left, BLOCK, BLOCK - reach)
        high = jnp.where(at_right, 2 * BLOCK, 2 * BLOCK + reach)
        extra = (high - low) % 2
        low = jnp.where(at_left, low, low - extra)
        high = jnp.where(at_left, high + extra, high)
        return low, high

    def messages(layer, x):
        slot = layer % 2
        centre = slice(GROUP, GROUP + NY)
        rows = []
        for d in range(2):
            for z in range(NZ):
                mid = norm_ref[slot, x + d, z, centre, :]
                total = norm_ref[slot, x + d - 1, z, centre, :] + norm_ref[slot, x + d + 1, z, centre, :]
                total = total + (
                    norm_ref[slot, x + d, z, :NY, :] + norm_ref[slot, x + d, z, 2 * GROUP :, :]
                )
                beside = [norm_ref[slot, x + d, w, centre, :] for w in (z - 1, z + 1) if 0 <= w < NZ]
                total = total + functools.reduce(lambda a, b: a + b, beside)
                rows.append(jnp.concatenate([mid, total], axis=-1))
        bias = bias_ref[layer]
        found = []
        for pair in rows:
            half = dot(pair, in_ref[layer]) + bias
            found.append((half * jnp.tanh(half) + half).astype(BF16))
        return found

    def keep(found):
        for at, message in enumerate(found):
            message_ref[at] = message

    def update(layer, x, held):
        for z in range(NZ):
            for d in range(2):
                message = held[d * NZ + z]
                moved = dot(jnp.concatenate([message, message], axis=-1), out_ref[layer])
                hidden = hidden_ref[x + d, z] + moved
                hidden_ref[x + d, z] = hidden
                store_normalized(layer + 1, x + d, z, hidden)

    def count(layer):
        low, high = rows_of(layer)
        return (high - low) // 2

    total = sum(count(layer) for layer in range(LAYERS))

    def advance(_, place):
        layer, x = place
        high = rows_of(layer)[1]
        ends = x + 2 >= high
        next_layer = jnp.where(ends, layer + 1, layer)
        next_x = jnp.where(ends, rows_of(layer + 1)[0], x + 2)
        held = [message_ref[at] for at in range(2 * NZ)]
        found = messages(next_layer, next_x)
        update(layer, x, held)
        keep(found)
        return next_layer, next_x

    start = (jnp.int32(0), rows_of(0)[0])
    keep(messages(*start))
    layer, x = lax.fori_loop(0, total - 1, advance, start)
    update(layer, x, [message_ref[at] for at in range(2 * NZ)])

    found = []
    for z in range(NZ):
        both = jnp.zeros((CHAN * BLOCK, NY), F32)
        for x in range(0, BLOCK, 2):
            pair = jnp.concatenate(
                [norm_ref[0, BLOCK + x + d, z, GROUP : GROUP + NY, :] for d in range(2)], axis=-1
            )
            both = both + dot_nt(dec_ref[x // 2], pair)
        found.append(both)
    change = dot(jnp.concatenate(found, axis=0), back_ref[...], precision=lax.Precision.HIGHEST)
    for c in range(CHAN):
        for z in range(NZ):
            at = (z * CHAN + c) * BLOCK
            state_ref[c, z] = own_ref[c, z] + change[at : at + BLOCK]
    send_ref[...] = state_ref[...].reshape(CHAN * NZ * BLOCK, NY).astype(BF16)


def run_fine_step(*args):
    vmem = pl.BlockSpec(memory_space=pltpu.VMEM)
    return pl.pallas_call(
        fine_step,
        out_shape=(
            jax.ShapeDtypeStruct((CHAN, NZ, BLOCK, NY), F32),
            jax.ShapeDtypeStruct((CHAN * NZ * BLOCK, NY), BF16),
        ),
        in_specs=[pl.BlockSpec(memory_space=pltpu.SMEM)] + [vmem] * 14,
        out_specs=(vmem, vmem),
        scratch_shapes=[
            pltpu.VMEM((FRAME, NZ, NY, HID), F32),
            pltpu.VMEM((2, FRAME, NZ, PADDED, HID), BF16),
            pltpu.VMEM((2 * NZ, NY, HID), BF16),
        ],
        compiler_params=pltpu.CompilerParams(vmem_limit_bytes=40 * 2**20),
        cost_estimate=pl.CostEstimate(flops=10**10, bytes_accessed=2**21, transcendentals=10**7),
        name="fine_step",
    )(*args)


def lookup_rate(sched_row, step_index, rate_values):
    picks = jnp.arange(RATES, dtype=jnp.int32) == sched_row[step_index]
    return jnp.sum(jnp.where(picks, rate_values, 0.0))


def centred(rows):
    return rows - jnp.mean(rows, axis=-1, keepdims=True)


def encoder(rate_value, enc_weight, type_table, force_vector):
    well = jnp.array([0.0, 1.0, -1.0], F32)[:, None] * rate_value * force_vector
    high, low = halves(centred(enc_weight))
    kind_high, kind_low = halves(centred(type_table + well))
    table = jnp.concatenate([high, high, low, kind_high, kind_low], axis=0)
    eye = jnp.eye(BLOCK, dtype=BF16)
    wide = table[:, None, None, :] * eye[None, :, :, None]
    return wide.reshape(FEATURES * BLOCK, BLOCK * HID)


def decoder(dec_weight):
    eye = jnp.eye(BLOCK, dtype=BF16)
    wide = dec_weight[:, None, None, :] * eye[None, :, :, None]
    wide = wide.reshape(CHAN * BLOCK, BLOCK // 2, 2 * HID)
    return wide.transpose(1, 0, 2)


def layer_weights(norm_gain, self_weight, neigh_weight, out_weight, layer_bias, dec_gain):
    enter = jnp.concatenate([self_weight, neigh_weight], axis=1) * jnp.asarray(0.5, BF16)
    leave = jnp.concatenate(halves(centred(out_weight.astype(F32))), axis=1)
    gains = jnp.concatenate([norm_gain, dec_gain[None]], axis=0)
    return enter, leave, (layer_bias * 0.5)[:, None, :], gains[:, None, :]


def exchange(value):
    count = lax.axis_size("space")
    first = [(i, i ^ 1) for i in range(count)]
    second = [(i, i + 1) for i in range(1, count - 1, 2)] + [(i + 1, i) for i in range(1, count - 1, 2)]
    return lax.ppermute(value, "space", first), lax.ppermute(value, "space", second)


def matvec(matrix, vector):
    return jnp.sum(matrix * vector[None], axis=1)


def matmat(left, right):
    return jnp.sum(left[:, :, None] * right[None], axis=1)


def per_device(
    prev_starts, plan, cell_type, coarse_matrix, rate_values, enc_weight, type_table, force_vector,
    norm_gain, self_weight, neigh_weight, out_weight, layer_bias, dec_gain, dec_weight,
):
    own = prev_starts[0]
    sched_row = plan[0]
    position = lax.axis_index("space")
    where = jnp.stack([position, lax.axis_size("space") - 1]).astype(jnp.int32)
    rows = CHAN * NZ * BLOCK

    outgoing = jnp.concatenate(
        [own.reshape(rows, NY).astype(BF16), cell_type.reshape(NZ * BLOCK, NY).astype(BF16)], axis=0
    )
    first, second = exchange(outgoing)
    kinds = [cell_type] + [side[rows:].astype(jnp.int32) for side in (first, second)]
    sides = [side[:rows].astype(F32) for side in (first, second)]

    enter, leave, bias, gains = layer_weights(
        norm_gain, self_weight, neigh_weight, out_weight, layer_bias, dec_gain
    )
    dec = decoder(dec_weight)
    order = jnp.asarray(TO_GROUPS, BF16)
    back = jnp.asarray(TO_GROUPS, F32)

    state = own
    for step_index in range(STEPS):
        rate_value = lookup_rate(sched_row, step_index, rate_values)
        enc = encoder(rate_value, enc_weight, type_table, force_vector)
        state, outgoing = run_fine_step(
            where, state, *sides, *kinds, enc, enter, leave, bias, gains, dec, order, back
        )
        if step_index + 1 < STEPS:
            sides = [side.astype(F32) for side in exchange(outgoing)]

    window = lax.axis_index("tm")
    total = jnp.where(window == 0, state, state - matvec(coarse_matrix, own))
    corrected = total
    power, reach = coarse_matrix, coarse_matrix
    count = lax.axis_size("tm")
    distance = 1
    while distance < count:
        came = lax.ppermute(total, "tm", [(i, i ^ distance) for i in range(count)])
        upper = (window // distance) % 2 == 1
        corrected = corrected + jnp.where(upper, matvec(reach, came), 0.0)
        if 2 * distance < count:
            lower_total = jnp.where(upper, came, total)
            upper_total = jnp.where(upper, total, came)
            total = upper_total + matvec(power, lower_total)
            reach = jnp.where(upper, matmat(power, reach), reach)
            power = matmat(power, power)
        distance *= 2
    return corrected[None]


def solution(mesh):
    return jax.shard_map(
        per_device,
        mesh=mesh,
        in_specs=(
            P("tm", None, None, "space", None),
            P("tm", None),
            P(None, "space", None),
            P(None, None, None, "space", None),
        )
        + (P(),) * 11,
        out_specs=P("tm", None, None, "space", None),
        check_vma=False,
    )
```

```python
import functools

import jax
import jax.numpy as jnp
import numpy as np
from jax import lax
from jax.experimental import pallas as pl
from jax.experimental.pallas import tpu as pltpu
from jax.sharding import PartitionSpec as P

HID = 128
CHAN = 4
NZ = 4
TYPES = 3
RATES = 8
LAYERS = 6
STEPS = 2
NY = 128

EPS = 1e-05

GROUPS, GROUP = 8, 16
PADDED = (GROUPS + 2) * GROUP
BLOCK = 8
FRAME = 3 * BLOCK
FEATURES = 3 * CHAN + 2 * TYPES

F32, BF16 = jnp.float32, jnp.bfloat16

_row = np.arange(NY)
TO_GROUPS = np.zeros((NY, NY), np.float32)
TO_GROUPS[_row, (_row % GROUP) * GROUPS + _row // GROUP] = 1.0


def dot(a, b, **kw):
    return jnp.dot(a, b, preferred_element_type=F32, **kw)


def dot_nt(a, b):
    return lax.dot_general(a, b, (((1,), (1,)), ((), ())), preferred_element_type=F32)


def halves(value):
    high = lax.reduce_precision(value, 8, 7)
    return high.astype(BF16), (value - high).astype(BF16)


def fine_step(
    where_ref, own_ref, first_ref, second_ref, kind_ref, kind_first_ref, kind_second_ref,
    enc_ref, in_ref, out_ref, bias_ref, gain_ref, dec_ref, order_ref, back_ref,
    state_ref, send_ref,
    hidden_ref, norm_ref, message_ref,
):
    position = where_ref[0]
    last = where_ref[1]
    odd = position % 2 == 1
    at_left = position == 0
    at_right = position == last

    def store_normalized(layer, x, z, hidden):
        slot = layer % 2
        square = jnp.sum(hidden * hidden, axis=-1, keepdims=True) * (1.0 / HID)
        normal = hidden * lax.rsqrt(square + EPS) * gain_ref[layer]
        norm_ref[slot, x, z, GROUP : GROUP + NY, :] = normal.astype(BF16)
        line = lax.broadcasted_iota(jnp.int32, (GROUP, HID), 0)
        before = pltpu.roll(normal[NY - GROUP :], 1, 0)
        before = jnp.where(line == 0, 0.0, before)
        norm_ref[slot, x, z, :GROUP, :] = before.astype(BF16)
        after = pltpu.roll(normal[:GROUP], GROUP - 1, 0)
        after = jnp.where(line == GROUP - 1, 0.0, after)
        norm_ref[slot, x, z, GROUP + NY :, :] = after.astype(BF16)

    @pl.when(at_left)
    def _():
        norm_ref[:, BLOCK - 1] = jnp.zeros((2, NZ, PADDED, HID), BF16)

    @pl.when(at_right)
    def _():
        norm_ref[:, 2 * BLOCK] = jnp.zeros((2, NZ, PADDED, HID), BF16)

    def encode(block, states, kinds, z):
        rows = []
        highs = [state.astype(BF16).astype(F32) for state in states]
        rows.extend(highs)
        rows.extend(state - high for state, high in zip(states, highs))
        rows.extend(highs)
        marks = [(kinds == kind).astype(F32) for kind in range(TYPES)]
        rows.extend(marks)
        rows.extend(marks)
        table = jnp.concatenate(rows, axis=0).astype(BF16)
        turned = dot_nt(order_ref[...], table).astype(BF16)
        for x in range(BLOCK):
            hidden = dot(turned, enc_ref[:, x * HID : (x + 1) * HID])
            hidden_ref[block * BLOCK + x, z] = hidden
            store_normalized(0, block * BLOCK + x, z, hidden)

    for z in range(NZ):
        encode(
            1,
            [own_ref[c, z] for c in range(CHAN)],
            kind_ref[z],
            z,
        )

    def neighbour(block, take_first):
        for z in range(NZ):
            states = []
            for c in range(CHAN):
                at = pl.ds((c * NZ + z) * BLOCK, BLOCK)
                states.append(jnp.where(take_first, first_ref[at, :], second_ref[at, :]))
            at = pl.ds(z * BLOCK, BLOCK)
            kinds = jnp.where(take_first, kind_first_ref[at, :], kind_second_ref[at, :])
            encode(block, states, kinds, z)

    @pl.when(jnp.logical_not(at_left))
    def _():
        neighbour(0, odd)

    @pl.when(jnp.logical_not(at_right))
    def _():
        neighbour(2, jnp.logical_not(odd))

    def rows_of(layer):
        reach = LAYERS - 1 - layer
        low = jnp.where(at_left, BLOCK, BLOCK - reach)
        high = jnp.where(at_right, 2 * BLOCK, 2 * BLOCK + reach)
        extra = (high - low) % 2
        low = jnp.where(at_left, low, low - extra)
        high = jnp.where(at_left, high + extra, high)
        return low, high

    def messages(layer, x):
        slot = layer % 2
        centre = slice(GROUP, GROUP + NY)
        rows = []
        for d in range(2):
            for z in range(NZ):
                mid = norm_ref[slot, x + d, z, centre, :]
                total = norm_ref[slot, x + d - 1, z, centre, :] + norm_ref[slot, x + d + 1, z, centre, :]
                total = total + (
                    norm_ref[slot, x + d, z, :NY, :] + norm_ref[slot, x + d, z, 2 * GROUP :, :]
                )
                beside = [norm_ref[slot, x + d, w, centre, :] for w in (z - 1, z + 1) if 0 <= w < NZ]
                total = total + functools.reduce(lambda a, b: a + b, beside)
                rows.append(jnp.concatenate([mid, total], axis=-1))
        bias = bias_ref[layer]
        found = []
        for pair in rows:
            half = dot(pair, in_ref[layer]) + bias
            found.append((half * jnp.tanh(half) + half).astype(BF16))
        return found

    def keep(found):
        for at, message in enumerate(found):
            message_ref[at] = message

    def update(layer, x, held):
        for z in range(NZ):
            for d in range(2):
                message = held[d * NZ + z]
                moved = dot(jnp.concatenate([message, message], axis=-1), out_ref[layer])
                hidden = hidden_ref[x + d, z] + moved
                hidden_ref[x + d, z] = hidden
                store_normalized(layer + 1, x + d, z, hidden)

    def count(layer):
        low, high = rows_of(layer)
        return (high - low) // 2

    total = sum(count(layer) for layer in range(LAYERS))

    def advance(_, place):
        layer, x = place
        high = rows_of(layer)[1]
        ends = x + 2 >= high
        next_layer = jnp.where(ends, layer + 1, layer)
        next_x = jnp.where(ends, rows_of(layer + 1)[0], x + 2)
        held = [message_ref[at] for at in range(2 * NZ)]
        found = messages(next_layer, next_x)
        update(layer, x, held)
        keep(found)
        return next_layer, next_x

    start = (jnp.int32(0), rows_of(0)[0])
    keep(messages(*start))
    layer, x = lax.fori_loop(0, total - 1, advance, start)
    update(layer, x, [message_ref[at] for at in range(2 * NZ)])

    found = []
    for z in range(NZ):
        both = jnp.zeros((CHAN * BLOCK, NY), F32)
        for x in range(0, BLOCK, 2):
            pair = jnp.concatenate(
                [norm_ref[0, BLOCK + x + d, z, GROUP : GROUP + NY, :] for d in range(2)], axis=-1
            )
            both = both + dot_nt(dec_ref[x // 2], pair)
        found.append(both)
    change = dot(jnp.concatenate(found, axis=0), back_ref[...], precision=lax.Precision.HIGHEST)
    for c in range(CHAN):
        for z in range(NZ):
            at = (z * CHAN + c) * BLOCK
            state_ref[c, z] = own_ref[c, z] + change[at : at + BLOCK]
    send_ref[...] = state_ref[...].reshape(CHAN * NZ * BLOCK, NY).astype(BF16)


def run_fine_step(*args):
    vmem = pl.BlockSpec(memory_space=pltpu.VMEM)
    return pl.pallas_call(
        fine_step,
        out_shape=(
            jax.ShapeDtypeStruct((CHAN, NZ, BLOCK, NY), F32),
            jax.ShapeDtypeStruct((CHAN * NZ * BLOCK, NY), BF16),
        ),
        in_specs=[pl.BlockSpec(memory_space=pltpu.SMEM)] + [vmem] * 14,
        out_specs=(vmem, vmem),
        scratch_shapes=[
            pltpu.VMEM((FRAME, NZ, NY, HID), F32),
            pltpu.VMEM((2, FRAME, NZ, PADDED, HID), BF16),
            pltpu.VMEM((2 * NZ, NY, HID), BF16),
        ],
        compiler_params=pltpu.CompilerParams(vmem_limit_bytes=40 * 2**20),
        cost_estimate=pl.CostEstimate(flops=10**10, bytes_accessed=2**21, transcendentals=10**7),
        name="fine_step",
    )(*args)


def lookup_rate(sched_row, step_index, rate_values):
    picks = jnp.arange(RATES, dtype=jnp.int32) == sched_row[step_index]
    return jnp.sum(jnp.where(picks, rate_values, 0.0))


def centred(rows):
    return rows - jnp.mean(rows, axis=-1, keepdims=True)


def encoder(rate_value, enc_weight, type_table, force_vector):
    well = jnp.array([0.0, 1.0, -1.0], F32)[:, None] * rate_value * force_vector
    high, low = halves(centred(enc_weight))
    kind_high, kind_low = halves(centred(type_table + well))
    table = jnp.concatenate([high, high, low, kind_high, kind_low], axis=0)
    eye = jnp.eye(BLOCK, dtype=BF16)
    wide = table[:, None, None, :] * eye[None, :, :, None]
    return wide.reshape(FEATURES * BLOCK, BLOCK * HID)


def decoder(dec_weight):
    eye = jnp.eye(BLOCK, dtype=BF16)
    wide = dec_weight[:, None, None, :] * eye[None, :, :, None]
    wide = wide.reshape(CHAN * BLOCK, BLOCK // 2, 2 * HID)
    return wide.transpose(1, 0, 2)


def layer_weights(norm_gain, self_weight, neigh_weight, out_weight, layer_bias, dec_gain):
    enter = jnp.concatenate([self_weight, neigh_weight], axis=1) * jnp.asarray(0.5, BF16)
    leave = jnp.concatenate(halves(centred(out_weight.astype(F32))), axis=1)
    gains = jnp.concatenate([norm_gain, dec_gain[None]], axis=0)
    return enter, leave, (layer_bias * 0.5)[:, None, :], gains[:, None, :]


def exchange(value):
    count = lax.axis_size("space")
    first = [(i, i ^ 1) for i in range(count)]
    second = [(i, i + 1) for i in range(1, count - 1, 2)] + [(i + 1, i) for i in range(1, count - 1, 2)]
    return lax.ppermute(value, "space", first), lax.ppermute(value, "space", second)


def matvec(matrix, vector):
    return jnp.sum(matrix * vector[None], axis=1)


def matmat(left, right):
    return jnp.sum(left[:, :, None] * right[None], axis=1)


def per_device(
    prev_starts, plan, cell_type, coarse_matrix, rate_values, enc_weight, type_table, force_vector,
    norm_gain, self_weight, neigh_weight, out_weight, layer_bias, dec_gain, dec_weight,
):
    own = prev_starts[0]
    sched_row = plan[0]
    position = lax.axis_index("space")
    where = jnp.stack([position, lax.axis_size("space") - 1]).astype(jnp.int32)
    rows = CHAN * NZ * BLOCK

    outgoing = jnp.concatenate(
        [own.reshape(rows, NY).astype(BF16), cell_type.reshape(NZ * BLOCK, NY).astype(BF16)], axis=0
    )
    first, second = exchange(outgoing)
    kinds = [cell_type] + [side[rows:].astype(jnp.int32) for side in (first, second)]
    sides = [side[:rows].astype(F32) for side in (first, second)]

    enter, leave, bias, gains = layer_weights(
        norm_gain, self_weight, neigh_weight, out_weight, layer_bias, dec_gain
    )
    dec = decoder(dec_weight)
    order = jnp.asarray(TO_GROUPS, BF16)
    back = jnp.asarray(TO_GROUPS, F32)

    state = own
    for step_index in range(STEPS):
        rate_value = lookup_rate(sched_row, step_index, rate_values)
        enc = encoder(rate_value, enc_weight, type_table, force_vector)
        state, outgoing = run_fine_step(
            where, state, *sides, *kinds, enc, enter, leave, bias, gains, dec, order, back
        )
        if step_index + 1 < STEPS:
            sides = [side.astype(F32) for side in exchange(outgoing)]

    window = lax.axis_index("tm")
    total = jnp.where(window == 0, state, state - matvec(coarse_matrix, own))
    corrected = total
    power, reach = coarse_matrix, coarse_matrix
    count = lax.axis_size("tm")
    distance = 1
    while distance < count:
        came = lax.ppermute(total, "tm", [(i, i ^ distance) for i in range(count)])
        upper = (window // distance) % 2 == 1
        corrected = corrected + jnp.where(upper, matvec(reach, came), 0.0)
        if 2 * distance < count:
            lower_total = jnp.where(upper, came, total)
            upper_total = jnp.where(upper, total, came)
            total = upper_total + matvec(power, lower_total)
            reach = jnp.where(upper, matmat(power, reach), reach)
            power = matmat(power, power)
        distance *= 2
    return corrected[None]


def solution(mesh):
    return jax.shard_map(
        per_device,
        mesh=mesh,
        in_specs=(
            P("tm", None, None, "space", None),
            P("tm", None),
            P(None, "space", None),
            P(None, None, None, "space", None),
        )
        + (P(),) * 11,
        out_specs=P("tm", None, None, "space", None),
        check_vma=False,
    )
```

```python
import functools

import jax
import jax.numpy as jnp
from jax import lax
from jax.experimental import pallas as pl
from jax.experimental.pallas import tpu as pltpu
from jax.sharding import PartitionSpec as P

HID = 128
CHAN = 4
NZ = 4
TYPES = 3
RATES = 8
LAYERS = 6
STEPS = 2
NY = 128

EPS = 1e-05

GROUPS, GROUP = 8, 16
PADDED = (GROUPS + 2) * GROUP
BLOCK = 8
FRAME = 3 * BLOCK
SPARE = FRAME + 2
HELD = SPARE + 3
FEATURES = 3 * CHAN + 2 * TYPES
ROWS = CHAN * NZ * BLOCK

F32, BF16 = jnp.float32, jnp.bfloat16


def dot(a, b, **kw):
    return jnp.dot(a, b, preferred_element_type=F32, **kw)


def dot_nt(a, b):
    return lax.dot_general(a, b, (((1,), (1,)), ((), ())), preferred_element_type=F32)


def grouped(dtype):
    row = lax.broadcasted_iota(jnp.int32, (NY, NY), 0)
    cell = lax.broadcasted_iota(jnp.int32, (NY, NY), 1)
    return (cell == (row % GROUP) * GROUPS + row // GROUP).astype(dtype)


def fine_step(
    where_ref, own_ref, first_ref, second_ref, kind_ref, kind_first_ref, kind_second_ref,
    enc_ref, in_ref, out_ref, bias_ref, gain_ref, dec_ref,
    state_ref, send_ref,
    hidden_ref, norm_ref, enter_ref,
):
    order = grouped(F32).astype(BF16)
    position = where_ref[0]
    last = where_ref[1]
    odd = position % 2 == 1
    at_left = position == 0
    at_right = position == last

    def strength(hidden):
        return jnp.sum(hidden * hidden, axis=-1, keepdims=True)

    def normalize(layer, hidden, target):
        normal = hidden * lax.rsqrt(strength(hidden) + HID * EPS) * gain_ref[layer]
        line = lax.broadcasted_iota(jnp.int32, (GROUP, HID), 0)
        before = jnp.where(line == 0, 0.0, pltpu.roll(normal[NY - GROUP :], 1, 0))
        after = jnp.where(line == GROUP - 1, 0.0, pltpu.roll(normal[:GROUP], GROUP - 1, 0))
        target[:GROUP, :] = before.astype(BF16)
        target[GROUP : GROUP + NY, :] = normal.astype(BF16)
        target[GROUP + NY :, :] = after.astype(BF16)

    @pl.when(at_left)
    def _():
        norm_ref[:, BLOCK - 1] = jnp.zeros((2, NZ, PADDED, HID), BF16)

    @pl.when(at_right)
    def _():
        norm_ref[:, 2 * BLOCK] = jnp.zeros((2, NZ, PADDED, HID), BF16)

    def encode(block, states, kinds, z):
        rows = []
        highs = [state.astype(BF16).astype(F32) for state in states]
        rows.extend(highs)
        rows.extend(state - high for state, high in zip(states, highs))
        rows.extend(highs)
        marks = [(kinds == float(kind)).astype(F32) for kind in range(TYPES)]
        rows.extend(marks)
        rows.extend(marks)
        table = jnp.concatenate(rows, axis=0).astype(BF16)
        turned = dot_nt(order, table).astype(BF16)
        for x in range(BLOCK):
            hidden = dot(turned, enc_ref[:, x * HID : (x + 1) * HID])
            hidden_ref[block * BLOCK + x, z] = hidden
            normalize(0, hidden, norm_ref.at[0, block * BLOCK + x, z])

    for z in range(NZ):
        encode(
            1,
            [own_ref[c, z] for c in range(CHAN)],
            kind_ref[z].astype(F32),
            z,
        )

    def neighbour(block, take_first):
        states = jnp.where(take_first, first_ref[:ROWS, :], second_ref[:ROWS, :]).astype(F32)
        kinds = jnp.where(take_first, kind_first_ref[ROWS:, :], kind_second_ref[ROWS:, :]).astype(F32)
        for z in range(NZ):
            parts = []
            for c in range(CHAN):
                at = (c * NZ + z) * BLOCK
                parts.append(states[at : at + BLOCK])
            encode(block, parts, kinds[z * BLOCK : (z + 1) * BLOCK], z)

    @pl.when(jnp.logical_not(at_left))
    def _():
        neighbour(0, odd)

    @pl.when(jnp.logical_not(at_right))
    def _():
        neighbour(2, jnp.logical_not(odd))

    def rows_of(layer):
        reach = LAYERS - 1 - layer
        low = jnp.where(at_left, BLOCK, BLOCK - reach)
        high = jnp.where(at_right, 2 * BLOCK, 2 * BLOCK + reach)
        return low, high

    tiles = [(d, z) for d in range(2) for z in range(NZ)]

    def group(start):
        return slice(start * GROUP, (start + 1) * GROUP)

    def gather(layer, x):
        slot = layer % 2
        loaded = {}

        def read(dx, z, start):
            if (dx, z, start) not in loaded:
                loaded[dx, z, start] = norm_ref[slot, x + dx, z, group(start), :]
            return loaded[dx, z, start]

        rows = []
        for start in range(1, GROUPS + 1):
            for d, z in tiles:
                along_x = read(d - 1, z, start) + read(d + 1, z, start)
                along_y = read(d, z, start - 1) + read(d, z, start + 1)
                beside = [read(d, w, start) for w in (z - 1, z + 1) if 0 <= w < NZ]
                along_z = functools.reduce(lambda a, b: a + b, beside)
                rows.append(jnp.concatenate([read(d, z, start), along_x + along_y + along_z], axis=-1))
        return jnp.concatenate(rows, axis=0)

    def turn(_, pairs):
        newest, second, third = pairs
        half = enter_ref[...]
        message = half * jnp.tanh(half) + half
        moved = dot(message, out_ref[second[0], :HID, :])
        entered = dot(gather(*newest), in_ref[newest[0]])
        enter_ref[...] = (entered + bias_ref[newest[0]]).astype(BF16)
        outside = jnp.logical_and(at_right, third[1] + 1 == 2 * BLOCK)
        slot = (third[0] + 1) % 2
        for d, z in tiles:
            row = third[1] if d == 0 else jnp.where(outside, SPARE, third[1] + 1)
            normalize(third[0] + 1, hidden_ref[third[1] + d, z], norm_ref.at[slot, row, z])
        for start in range(GROUPS):
            for at, (d, z) in enumerate(tiles):
                part = moved[group(start * len(tiles) + at)]
                hidden_ref[second[1] + d, z, group(start), :] += part
        layer, x = newest
        ends = x + 2 >= rows_of(layer)[1]
        next_layer = jnp.where(ends, layer + 1, layer)
        next_x = jnp.where(ends, rows_of(layer + 1)[0], x + 2)
        done = next_layer >= LAYERS
        following = (jnp.where(done, 0, next_layer), jnp.where(done, SPARE, next_x))
        return following, newest, second

    def count(layer):
        low, high = rows_of(layer)
        return (high - low + 1) // 2

    total = sum(count(layer) for layer in range(LAYERS))
    none = (jnp.int32(0), jnp.int32(SPARE))
    start = (jnp.int32(0), rows_of(0)[0])
    lax.fori_loop(0, total + 2, turn, (start, none, none))

    found = []
    for z in range(NZ):
        both = jnp.zeros((CHAN * BLOCK, NY), F32)
        for x in range(0, BLOCK, 2):
            pair = jnp.concatenate(
                [norm_ref[0, BLOCK + x + d, z, GROUP : GROUP + NY, :] for d in range(2)], axis=-1
            )
            both = both + dot_nt(dec_ref[x // 2], pair)
        found.append(both)
    change = dot(jnp.concatenate(found, axis=0), grouped(F32), precision=lax.Precision.HIGHEST)
    for c in range(CHAN):
        for z in range(NZ):
            at = (z * CHAN + c) * BLOCK
            state_ref[c, z] = own_ref[c, z] + change[at : at + BLOCK]
    send_ref[...] = state_ref[...].reshape(CHAN * NZ * BLOCK, NY).astype(BF16)


def run_fine_step(*args):
    vmem = pl.BlockSpec(memory_space=pltpu.VMEM)
    return pl.pallas_call(
        fine_step,
        out_shape=(
            jax.ShapeDtypeStruct((CHAN, NZ, BLOCK, NY), F32),
            jax.ShapeDtypeStruct((CHAN * NZ * BLOCK, NY), BF16),
        ),
        in_specs=[pl.BlockSpec(memory_space=pltpu.SMEM)] + [vmem] * 12,
        out_specs=(vmem, vmem),
        scratch_shapes=[
            pltpu.VMEM((HELD, NZ, NY, HID), F32),
            pltpu.VMEM((2, HELD, NZ, PADDED, HID), BF16),
            pltpu.VMEM((2 * NZ * NY, HID), BF16),
        ],
        compiler_params=pltpu.CompilerParams(vmem_limit_bytes=40 * 2**20),
        cost_estimate=pl.CostEstimate(flops=10**10, bytes_accessed=2**21, transcendentals=10**7),
        name="fine_step",
    )(*args)


def centred(rows):
    return rows - jnp.mean(rows, axis=-1, keepdims=True)


def halves(value):
    high = value.astype(BF16)
    return high, (value - high.astype(F32)).astype(BF16)


def prepare(
    plan_ref, rate_ref,
    enc_hbm, type_hbm, force_hbm, gain_hbm, self_hbm, neigh_hbm, out_hbm, bias_hbm, dec_gain_hbm, dec_hbm,
    enc_first_ref, enc_second_ref, in_ref, leave_ref, bias_ref, gains_ref, dec_out_ref,
    enc, kind, force, gain, own, neigh, out, bias, dec_gain, dec, sems,
):
    sources = (enc_hbm, type_hbm, force_hbm, gain_hbm, self_hbm, neigh_hbm, out_hbm, bias_hbm, dec_gain_hbm, dec_hbm)
    targets = (enc, kind, force, gain, own, neigh, out, bias, dec_gain, dec)
    copies = [pltpu.make_async_copy(a, b, sems.at[n]) for n, (a, b) in enumerate(zip(sources, targets))]
    for copy in copies:
        copy.start()
    for copy in copies:
        copy.wait()

    line = lax.broadcasted_iota(jnp.int32, (BLOCK, HID), 0)

    def spread(rows, x):
        return [jnp.where(line == x, row, 0.0) for row in rows]

    weights = halves(centred(enc[...]))
    for step, enc_ref in enumerate((enc_first_ref, enc_second_ref)):
        rate = rate_ref[plan_ref[0, step]]
        push = rate * force[...]
        table = kind[...]
        kinds = halves(centred(jnp.concatenate([table[0:1], table[1:2] + push, table[2:3] - push], axis=0)))
        high, low = [half.astype(F32) for half in weights]
        rows = [part[c : c + 1] for part in (high, high, low) for c in range(CHAN)]
        rows += [part.astype(F32)[k : k + 1] for part in kinds for k in range(TYPES)]
        for x in range(BLOCK):
            enc_ref[:, x * HID : (x + 1) * HID] = jnp.concatenate(spread(rows, x), axis=0).astype(BF16)
    for layer in range(LAYERS):
        half = jnp.asarray(0.5, BF16)
        in_ref[layer, :HID, :] = own[layer] * half
        in_ref[layer, HID:, :] = neigh[layer] * half
        high, low = halves(centred(out[layer].astype(F32)))
        leave_ref[layer, :HID, :] = high
        leave_ref[layer, HID:, :] = low
        bias_ref[layer] = bias[layer : layer + 1, :] * 0.5
        gains_ref[layer] = gain[layer : layer + 1, :] * HID**0.5
    gains_ref[LAYERS] = dec_gain[...] * HID**0.5
    rows = [dec[...].astype(F32)[c : c + 1] for c in range(CHAN)]
    for x in range(BLOCK):
        part = jnp.concatenate(spread(rows, x), axis=0).astype(BF16)
        dec_out_ref[x // 2, :, (x % 2) * HID : (x % 2 + 1) * HID] = part


def run_prepare(plan, rate_values, *arrays):
    vmem = pl.BlockSpec(memory_space=pltpu.VMEM)
    smem = pl.BlockSpec(memory_space=pltpu.SMEM)
    shapes = (
        ((FEATURES * BLOCK, BLOCK * HID), BF16),
        ((FEATURES * BLOCK, BLOCK * HID), BF16),
        ((LAYERS, 2 * HID, HID), BF16),
        ((LAYERS, 2 * HID, HID), BF16),
        ((LAYERS, 1, HID), F32),
        ((LAYERS + 1, 1, HID), F32),
        ((BLOCK // 2, CHAN * BLOCK, 2 * HID), BF16),
    )
    return pl.pallas_call(
        prepare,
        out_shape=tuple(jax.ShapeDtypeStruct(shape, dtype) for shape, dtype in shapes),
        in_specs=[smem] * 2 + [pl.BlockSpec(memory_space=pl.ANY)] * len(arrays),
        out_specs=(vmem,) * len(shapes),
        scratch_shapes=[pltpu.VMEM(array.shape, array.dtype) for array in arrays]
        + [pltpu.SemaphoreType.DMA((len(arrays),))],
        compiler_params=pltpu.CompilerParams(vmem_limit_bytes=16 * 2**20),
        cost_estimate=pl.CostEstimate(flops=10**8, bytes_accessed=2**21, transcendentals=0),
        name="prepare",
    )(plan, rate_values, *arrays)


def exchange(value):
    count = lax.axis_size("space")
    first = [(i, i ^ 1) for i in range(count)]
    second = [(i, i + 1) for i in range(1, count - 1, 2)] + [(i + 1, i) for i in range(1, count - 1, 2)]
    return lax.ppermute(value, "space", first), lax.ppermute(value, "space", second)


def matvec(matrix, vector):
    return jnp.sum(matrix * vector[None], axis=1)


def matmat(left, right):
    return jnp.sum(left[:, :, None] * right[None], axis=1)


def per_device(
    prev_starts, plan, cell_type, coarse_matrix, rate_values, enc_weight, type_table, force_vector,
    norm_gain, self_weight, neigh_weight, out_weight, layer_bias, dec_gain, dec_weight,
):
    own = prev_starts[0]
    position = lax.axis_index("space")
    where = jnp.stack([position, lax.axis_size("space") - 1]).astype(jnp.int32)

    outgoing = jnp.concatenate(
        [own.reshape(ROWS, NY).astype(BF16), cell_type.reshape(NZ * BLOCK, NY).astype(BF16)], axis=0
    )
    kinds = sides = exchange(outgoing)
    enc_first, enc_second, *weights = run_prepare(
        plan, rate_values, enc_weight, type_table, force_vector[None], norm_gain, self_weight,
        neigh_weight, out_weight, layer_bias, dec_gain[None], dec_weight,
    )

    state = own
    for step_index in range(STEPS):
        state, outgoing = run_fine_step(
            where, state, *sides, cell_type, *kinds, (enc_first, enc_second)[step_index], *weights
        )
        if step_index + 1 < STEPS:
            sides = exchange(outgoing)

    window = lax.axis_index("tm")
    total = jnp.where(window == 0, state, state - matvec(coarse_matrix, own))
    corrected = total
    power, reach = coarse_matrix, coarse_matrix
    count = lax.axis_size("tm")
    distance = 1
    while distance < count:
        came = lax.ppermute(total.astype(BF16), "tm", [(i, i ^ distance) for i in range(count)])
        came = came.astype(F32)
        upper = (window // distance) % 2 == 1
        corrected = corrected + jnp.where(upper, matvec(reach, came), 0.0)
        if 2 * distance < count:
            lower_total = jnp.where(upper, came, total)
            upper_total = jnp.where(upper, total, came)
            total = upper_total + matvec(power, lower_total)
            reach = jnp.where(upper, matmat(power, reach), reach)
            power = matmat(power, power)
        distance *= 2
    return corrected[None]


def solution(mesh):
    return jax.shard_map(
        per_device,
        mesh=mesh,
        in_specs=(
            P("tm", None, None, "space", None),
            P("tm", None),
            P(None, "space", None),
            P(None, None, None, "space", None),
        )
        + (P(),) * 11,
        out_specs=P("tm", None, None, "space", None),
        check_vma=False,
    )
```

```python
import functools

import jax
import jax.numpy as jnp
from jax import lax
from jax.experimental import pallas as pl
from jax.experimental.pallas import tpu as pltpu
from jax.sharding import PartitionSpec as P

HID = 128
CHAN = 4
NZ = 4
TYPES = 3
RATES = 8
LAYERS = 6
STEPS = 2
NY = 128

EPS = 1e-05

GROUPS, GROUP = 8, 16
PADDED = (GROUPS + 2) * GROUP
BLOCK = 8
FRAME = 3 * BLOCK
SPARE = FRAME + 2
HELD = SPARE + 3
FEATURES = 2 * CHAN + 2 * TYPES
ROWS = CHAN * NZ * BLOCK

SWAPS = {1: 1, 2: 2, 4: 6, 8: 8, 16: 24}

F32, BF16 = jnp.float32, jnp.bfloat16


def dot(a, b, **kw):
    return jnp.dot(a, b, preferred_element_type=F32, **kw)


def dot_nt(a, b):
    return lax.dot_general(a, b, (((1,), (1,)), ((), ())), preferred_element_type=F32)


def grouped(dtype):
    row = lax.broadcasted_iota(jnp.int32, (NY, NY), 0)
    cell = lax.broadcasted_iota(jnp.int32, (NY, NY), 1)
    return (cell == (row % GROUP) * GROUPS + row // GROUP).astype(dtype)


def fine_step(
    where_ref, own_ref, first_ref, second_ref, kind_ref, kind_first_ref, kind_second_ref,
    enc_ref, in_ref, out_ref, bias_ref, gain_ref, dec_ref,
    state_ref, send_ref,
    hidden_ref, norm_ref, enter_ref,
):
    order = grouped(F32).astype(BF16)
    position = where_ref[0]
    last = where_ref[1]
    odd = position % 2 == 1
    at_left = position == 0
    at_right = position == last

    def strength(hidden):
        return jnp.sum(hidden * hidden, axis=-1, keepdims=True)

    def normalize(layer, hidden, target):
        normal = hidden * lax.rsqrt(strength(hidden) + HID * EPS) * gain_ref[layer]
        line = lax.broadcasted_iota(jnp.int32, (GROUP, HID), 0)
        before = jnp.where(line == 0, 0.0, pltpu.roll(normal[NY - GROUP :], 1, 0))
        after = jnp.where(line == GROUP - 1, 0.0, pltpu.roll(normal[:GROUP], GROUP - 1, 0))
        target[:GROUP, :] = before.astype(BF16)
        target[GROUP : GROUP + NY, :] = normal.astype(BF16)
        target[GROUP + NY :, :] = after.astype(BF16)

    @pl.when(at_left)
    def _():
        norm_ref[:, BLOCK - 1] = jnp.zeros((2, NZ, PADDED, HID), BF16)

    @pl.when(at_right)
    def _():
        norm_ref[:, 2 * BLOCK] = jnp.zeros((2, NZ, PADDED, HID), BF16)

    def encode(block, states, kinds, xs):
        turned = []
        for z in range(NZ):
            rows = [states[(c * NZ + z) * BLOCK : (c * NZ + z + 1) * BLOCK] for c in range(CHAN)]
            kind_row = kinds[z * BLOCK : (z + 1) * BLOCK]
            marks = [(kind_row == float(kind)).astype(F32) for kind in range(TYPES)]
            table = jnp.concatenate(rows + rows + marks + marks, axis=0).astype(BF16)
            turned.append(dot_nt(order, table).astype(BF16))
        turned = jnp.concatenate(turned, axis=0)
        for first in range(xs.start, xs.stop, 2):
            found = dot(turned, enc_ref[:, first * HID : (first + 2) * HID])
            for x in (first, first + 1):
                for z in range(NZ):
                    hidden = found[z * NY : (z + 1) * NY, (x - first) * HID : (x - first + 1) * HID]
                    hidden_ref[block * BLOCK + x, z] = hidden
                    normalize(0, hidden, norm_ref.at[0, block * BLOCK + x, z])

    encode(1, own_ref[...].reshape(ROWS, NY), kind_ref[...].reshape(NZ * BLOCK, NY).astype(F32), range(BLOCK))

    def neighbour(block, take_first, xs):
        states = jnp.where(take_first, first_ref[:ROWS, :], second_ref[:ROWS, :]).astype(F32)
        kinds = jnp.where(take_first, kind_first_ref[ROWS:, :], kind_second_ref[ROWS:, :]).astype(F32)
        encode(block, states, kinds, xs)

    @pl.when(jnp.logical_not(at_left))
    def _():
        neighbour(0, odd, range(BLOCK - LAYERS, BLOCK))

    @pl.when(jnp.logical_not(at_right))
    def _():
        neighbour(2, jnp.logical_not(odd), range(LAYERS))

    def rows_of(layer):
        reach = LAYERS - 1 - layer
        low = jnp.where(at_left, BLOCK, BLOCK - reach)
        high = jnp.where(at_right, 2 * BLOCK, 2 * BLOCK + reach)
        return low, high

    tiles = [(d, z) for d in range(2) for z in range(NZ)]

    def group(start):
        return slice(start * GROUP, (start + 1) * GROUP)

    def gather(layer, x):
        slot = layer % 2
        loaded = {}

        def read(dx, z, start):
            if (dx, z, start) not in loaded:
                loaded[dx, z, start] = norm_ref[slot, x + dx, z, group(start), :]
            return loaded[dx, z, start]

        rows = []
        for start in range(1, GROUPS + 1):
            for d, z in tiles:
                along_x = read(d - 1, z, start) + read(d + 1, z, start)
                along_y = read(d, z, start - 1) + read(d, z, start + 1)
                beside = [read(d, w, start) for w in (z - 1, z + 1) if 0 <= w < NZ]
                along_z = functools.reduce(lambda a, b: a + b, beside)
                rows.append(jnp.concatenate([read(d, z, start), along_x + along_y + along_z], axis=-1))
        return jnp.concatenate(rows, axis=0)

    def turn(_, pairs):
        newest, second, third = pairs
        half = enter_ref[...]
        message = half * jnp.tanh(half) + half
        moved = dot(message, out_ref[second[0]])
        entered = dot(gather(*newest), in_ref[newest[0]])
        enter_ref[...] = (entered + bias_ref[newest[0]]).astype(BF16)
        outside = jnp.logical_and(at_right, third[1] + 1 == 2 * BLOCK)
        slot = (third[0] + 1) % 2
        for d, z in tiles:
            row = third[1] if d == 0 else jnp.where(outside, SPARE, third[1] + 1)
            normalize(third[0] + 1, hidden_ref[third[1] + d, z], norm_ref.at[slot, row, z])
        for start in range(GROUPS):
            for at, (d, z) in enumerate(tiles):
                part = moved[group(start * len(tiles) + at)]
                hidden_ref[second[1] + d, z, group(start), :] += part
        layer, x = newest
        ends = x + 2 >= rows_of(layer)[1]
        next_layer = jnp.where(ends, layer + 1, layer)
        next_x = jnp.where(ends, rows_of(layer + 1)[0], x + 2)
        done = next_layer >= LAYERS
        following = (jnp.where(done, 0, next_layer), jnp.where(done, SPARE, next_x))
        return following, newest, second

    def count(layer):
        low, high = rows_of(layer)
        return (high - low + 1) // 2

    total = sum(count(layer) for layer in range(LAYERS))
    none = (jnp.int32(0), jnp.int32(SPARE))
    start = (jnp.int32(0), rows_of(0)[0])
    lax.fori_loop(0, total + 2, turn, (start, none, none))

    found = []
    for z in range(NZ):
        both = jnp.zeros((CHAN * BLOCK, NY), F32)
        for x in range(0, BLOCK, 2):
            pair = jnp.concatenate(
                [norm_ref[0, BLOCK + x + d, z, GROUP : GROUP + NY, :] for d in range(2)], axis=-1
            )
            both = both + dot_nt(dec_ref[x // 2], pair)
        found.append(both)
    change = dot(jnp.concatenate(found, axis=0), grouped(F32), precision=lax.Precision.HIGHEST)
    for c in range(CHAN):
        for z in range(NZ):
            at = (z * CHAN + c) * BLOCK
            state_ref[c, z] = own_ref[c, z] + change[at : at + BLOCK]
    send_ref[...] = state_ref[...].reshape(CHAN * NZ * BLOCK, NY).astype(BF16)


def run_fine_step(*args):
    vmem = pl.BlockSpec(memory_space=pltpu.VMEM)
    return pl.pallas_call(
        fine_step,
        out_shape=(
            jax.ShapeDtypeStruct((CHAN, NZ, BLOCK, NY), F32),
            jax.ShapeDtypeStruct((CHAN * NZ * BLOCK, NY), BF16),
        ),
        in_specs=[pl.BlockSpec(memory_space=pltpu.SMEM)] + [vmem] * 12,
        out_specs=(vmem, vmem),
        scratch_shapes=[
            pltpu.VMEM((HELD, NZ, NY, HID), F32),
            pltpu.VMEM((2, HELD, NZ, PADDED, HID), BF16),
            pltpu.VMEM((2 * NZ * NY, HID), BF16),
        ],
        compiler_params=pltpu.CompilerParams(vmem_limit_bytes=40 * 2**20),
        cost_estimate=pl.CostEstimate(flops=10**10, bytes_accessed=2**21, transcendentals=10**7),
        name="fine_step",
    )(*args)


def centred(rows):
    return rows - jnp.mean(rows, axis=-1, keepdims=True)


def halves(value):
    high = value.astype(BF16)
    return high, (value - high.astype(F32)).astype(BF16)


def prepare(
    plan_ref, rate_ref,
    enc_hbm, type_hbm, force_hbm, gain_hbm, self_hbm, neigh_hbm, out_hbm, bias_hbm, dec_gain_hbm, dec_hbm,
    enc_first_ref, enc_second_ref, in_ref, leave_ref, bias_ref, gains_ref, dec_out_ref,
    enc, kind, force, gain, own, neigh, out, bias, dec_gain, dec, sems,
):
    sources = (enc_hbm, type_hbm, force_hbm, gain_hbm, self_hbm, neigh_hbm, out_hbm, bias_hbm, dec_gain_hbm, dec_hbm)
    targets = (enc, kind, force, gain, own, neigh, out, bias, dec_gain, dec)
    copies = [pltpu.make_async_copy(a, b, sems.at[n]) for n, (a, b) in enumerate(zip(sources, targets))]
    for copy in copies:
        copy.start()
    for copy in copies:
        copy.wait()

    line = lax.broadcasted_iota(jnp.int32, (BLOCK, HID), 0)

    def spread(rows, x):
        return [jnp.where(line == x, row, 0.0) for row in rows]

    weights = halves(centred(enc[...]))
    for step, enc_ref in enumerate((enc_first_ref, enc_second_ref)):
        rate = rate_ref[plan_ref[0, step]]
        push = rate * force[...]
        table = kind[...]
        kinds = halves(centred(jnp.concatenate([table[0:1], table[1:2] + push, table[2:3] - push], axis=0)))
        high, low = [half.astype(F32) for half in weights]
        rows = [part[c : c + 1] for part in (high, low) for c in range(CHAN)]
        rows += [part.astype(F32)[k : k + 1] for part in kinds for k in range(TYPES)]
        for x in range(BLOCK):
            enc_ref[:, x * HID : (x + 1) * HID] = jnp.concatenate(spread(rows, x), axis=0).astype(BF16)
    for layer in range(LAYERS):
        half = jnp.asarray(0.5, BF16)
        in_ref[layer, :HID, :] = own[layer] * half
        in_ref[layer, HID:, :] = neigh[layer] * half
        leave_ref[layer] = centred(out[layer].astype(F32)).astype(BF16)
        bias_ref[layer] = bias[layer : layer + 1, :] * 0.5
        gains_ref[layer] = gain[layer : layer + 1, :] * HID**0.5
    gains_ref[LAYERS] = dec_gain[...] * HID**0.5
    rows = [dec[...].astype(F32)[c : c + 1] for c in range(CHAN)]
    for x in range(BLOCK):
        part = jnp.concatenate(spread(rows, x), axis=0).astype(BF16)
        dec_out_ref[x // 2, :, (x % 2) * HID : (x % 2 + 1) * HID] = part


def run_prepare(plan, rate_values, *arrays):
    vmem = pl.BlockSpec(memory_space=pltpu.VMEM)
    smem = pl.BlockSpec(memory_space=pltpu.SMEM)
    shapes = (
        ((FEATURES * BLOCK, BLOCK * HID), BF16),
        ((FEATURES * BLOCK, BLOCK * HID), BF16),
        ((LAYERS, 2 * HID, HID), BF16),
        ((LAYERS, HID, HID), BF16),
        ((LAYERS, 1, HID), F32),
        ((LAYERS + 1, 1, HID), F32),
        ((BLOCK // 2, CHAN * BLOCK, 2 * HID), BF16),
    )
    return pl.pallas_call(
        prepare,
        out_shape=tuple(jax.ShapeDtypeStruct(shape, dtype) for shape, dtype in shapes),
        in_specs=[smem] * 2 + [pl.BlockSpec(memory_space=pltpu.HBM)] * len(arrays),
        out_specs=(vmem,) * len(shapes),
        scratch_shapes=[pltpu.VMEM(array.shape, array.dtype) for array in arrays]
        + [pltpu.SemaphoreType.DMA((len(arrays),))],
        compiler_params=pltpu.CompilerParams(vmem_limit_bytes=16 * 2**20),
        cost_estimate=pl.CostEstimate(flops=10**8, bytes_accessed=2**21, transcendentals=0),
        name="prepare",
    )(plan, rate_values, *arrays)


def exchange(value):
    count = lax.axis_size("space")
    first = [(i, i ^ 1) for i in range(count)]
    second = [(i, i + 1) for i in range(1, count - 1, 2)] + [(i + 1, i) for i in range(1, count - 1, 2)]
    return lax.ppermute(value, "space", first), lax.ppermute(value, "space", second)


def matvec(matrix, vector):
    return jnp.sum(matrix * vector[None], axis=1)


def matmat(left, right):
    return jnp.sum(left[:, :, None] * right[None], axis=1)


def per_device(
    prev_starts, plan, cell_type, coarse_matrix, rate_values, enc_weight, type_table, force_vector,
    norm_gain, self_weight, neigh_weight, out_weight, layer_bias, dec_gain, dec_weight,
):
    own = prev_starts[0]
    position = lax.axis_index("space")
    where = jnp.stack([position, lax.axis_size("space") - 1]).astype(jnp.int32)

    outgoing = jnp.concatenate(
        [own.reshape(ROWS, NY).astype(BF16), cell_type.reshape(NZ * BLOCK, NY).astype(BF16)], axis=0
    )
    kinds = sides = exchange(outgoing)
    enc_first, enc_second, *weights = run_prepare(
        plan, rate_values, enc_weight, type_table, force_vector[None], norm_gain, self_weight,
        neigh_weight, out_weight, layer_bias, dec_gain[None], dec_weight,
    )

    state = own
    for step_index in range(STEPS):
        state, outgoing = run_fine_step(
            where, state, *sides, cell_type, *kinds, (enc_first, enc_second)[step_index], *weights
        )
        if step_index + 1 < STEPS:
            sides = exchange(outgoing)

    window = lax.axis_index("tm")
    total = jnp.where(window == 0, state, state - matvec(coarse_matrix, own))
    corrected = total
    power, reach = coarse_matrix, coarse_matrix
    count = lax.axis_size("tm")
    distance = 1
    while distance < count:
        partners = [(i, i ^ SWAPS[distance]) for i in range(count)]
        came = lax.ppermute(total.astype(jnp.float16), "tm", partners).astype(F32)
        upper = (window // distance) % 2 == 1
        corrected = corrected + jnp.where(upper, matvec(reach, came), 0.0)
        if 2 * distance < count:
            lower_total = jnp.where(upper, came, total)
            upper_total = jnp.where(upper, total, came)
            total = upper_total + matvec(power, lower_total)
            reach = jnp.where(upper, matmat(power, reach), reach)
            power = matmat(power, power)
        distance *= 2
    return corrected[None]


def solution(mesh):
    return jax.shard_map(
        per_device,
        mesh=mesh,
        in_specs=(
            P("tm", None, None, "space", None),
            P("tm", None),
            P(None, "space", None),
            P(None, None, None, "space", None),
        )
        + (P(),) * 11,
        out_specs=P("tm", None, None, "space", None),
        check_vma=False,
    )
```

```python
import functools

import jax
import jax.numpy as jnp
from jax import lax
from jax.experimental import pallas as pl
from jax.experimental.pallas import tpu as pltpu
from jax.sharding import PartitionSpec as P

HID = 128
CHAN = 4
NZ = 4
TYPES = 3
RATES = 8
LAYERS = 6
STEPS = 2
NY = 128

EPS = 1e-05

GROUPS, GROUP = 8, 16
PADDED = (GROUPS + 2) * GROUP
BLOCK = 8
FRAME = 3 * BLOCK
SPARE = FRAME + 2
HELD = SPARE + 3
FEATURES = 2 * CHAN + 2 * TYPES
ROWS = CHAN * NZ * BLOCK

SWAPS = {1: 1, 2: 2, 4: 6, 8: 8, 16: 24}

F32, BF16 = jnp.float32, jnp.bfloat16


def dot(a, b, **kw):
    return jnp.dot(a, b, preferred_element_type=F32, **kw)


def dot_nt(a, b):
    return lax.dot_general(a, b, (((1,), (1,)), ((), ())), preferred_element_type=F32)


def grouped(dtype):
    row = lax.broadcasted_iota(jnp.int32, (NY, NY), 0)
    cell = lax.broadcasted_iota(jnp.int32, (NY, NY), 1)
    return (cell == (row % GROUP) * GROUPS + row // GROUP).astype(dtype)


def fine_step(
    where_ref, own_ref, first_ref, second_ref, kind_ref, kind_first_ref, kind_second_ref,
    enc_ref, self_ref, neigh_ref, out_ref, bias_ref, gain_ref, dec_ref,
    state_ref, send_ref,
    hidden_ref, norm_ref, enter_ref,
):
    order = grouped(F32).astype(BF16)
    position = where_ref[0]
    last = where_ref[1]
    odd = position % 2 == 1
    at_left = position == 0
    at_right = position == last

    def strength(hidden):
        return jnp.sum(hidden * hidden, axis=-1, keepdims=True)

    def normalize(layer, hidden, target):
        normal = hidden * lax.rsqrt(strength(hidden) + HID * EPS) * gain_ref[layer]
        line = lax.broadcasted_iota(jnp.int32, (GROUP, HID), 0)
        before = jnp.where(line == 0, 0.0, pltpu.roll(normal[NY - GROUP :], 1, 0))
        after = jnp.where(line == GROUP - 1, 0.0, pltpu.roll(normal[:GROUP], GROUP - 1, 0))
        target[:GROUP, :] = before.astype(BF16)
        target[GROUP : GROUP + NY, :] = normal.astype(BF16)
        target[GROUP + NY :, :] = after.astype(BF16)

    @pl.when(at_left)
    def _():
        norm_ref[:, BLOCK - 1] = jnp.zeros((2, NZ, PADDED, HID), BF16)

    @pl.when(at_right)
    def _():
        norm_ref[:, 2 * BLOCK] = jnp.zeros((2, NZ, PADDED, HID), BF16)

    def encode(block, states, kinds, xs):
        turned = []
        for z in range(NZ):
            rows = [states[(c * NZ + z) * BLOCK : (c * NZ + z + 1) * BLOCK] for c in range(CHAN)]
            kind_row = kinds[z * BLOCK : (z + 1) * BLOCK]
            marks = [(kind_row == float(kind)).astype(F32) for kind in range(TYPES)]
            table = jnp.concatenate(rows + rows + marks + marks, axis=0).astype(BF16)
            turned.append(dot_nt(order, table).astype(BF16))
        turned = jnp.concatenate(turned, axis=0)
        for first in range(xs.start, xs.stop, 2):
            found = dot(turned, enc_ref[:, first * HID : (first + 2) * HID])
            for x in (first, first + 1):
                for z in range(NZ):
                    hidden = found[z * NY : (z + 1) * NY, (x - first) * HID : (x - first + 1) * HID]
                    hidden_ref[block * BLOCK + x, z] = hidden
                    normalize(0, hidden, norm_ref.at[0, block * BLOCK + x, z])

    encode(1, own_ref[...].reshape(ROWS, NY), kind_ref[...].reshape(NZ * BLOCK, NY).astype(F32), range(BLOCK))

    def neighbour(block, take_first, xs):
        states = jnp.where(take_first, first_ref[:ROWS, :], second_ref[:ROWS, :]).astype(F32)
        kinds = jnp.where(take_first, kind_first_ref[ROWS:, :], kind_second_ref[ROWS:, :]).astype(F32)
        encode(block, states, kinds, xs)

    @pl.when(jnp.logical_not(at_left))
    def _():
        neighbour(0, odd, range(BLOCK - LAYERS, BLOCK))

    @pl.when(jnp.logical_not(at_right))
    def _():
        neighbour(2, jnp.logical_not(odd), range(LAYERS))

    def rows_of(layer):
        reach = LAYERS - 1 - layer
        low = jnp.where(at_left, BLOCK, BLOCK - reach)
        high = jnp.where(at_right, 2 * BLOCK, 2 * BLOCK + reach)
        return low, high

    tiles = [(d, z) for d in range(2) for z in range(NZ)]

    def group(start):
        return slice(start * GROUP, (start + 1) * GROUP)

    def gather(layer, x):
        slot = layer % 2
        loaded = {}

        def read(dx, z, start, own=None):
            loaded_key = (dx, z, start, own)
            if loaded_key not in loaded:
                loaded[loaded_key] = norm_ref[slot, x + dx, z, group(start), :]
            return loaded[loaded_key]

        rows = []
        for d, z in tiles:
            for start in range(1, GROUPS + 1):
                key = (d, z)
                mid = read(d, z, start, key)
                along_x = read(d - 1, z, start, (key, 1)) + read(d + 1, z, start, (key, 1))
                along_y = read(d, z, start - 1, key) + read(d, z, start + 1, key)
                beside = [read(d, w, start, (key, 2)) for w in (z - 1, z + 1) if 0 <= w < NZ]
                along_z = functools.reduce(lambda a, b: a + b, beside)
                rows.append(jnp.concatenate([mid, along_x + along_y + along_z], axis=-1))
        return jnp.concatenate(rows, axis=0)

    def turn(_, pairs):
        newest, second, third = pairs
        half = enter_ref[...]
        message = half * jnp.tanh(half) + half
        moved = dot(jnp.concatenate([message, message], axis=-1), out_ref[second[0]])
        enter = jnp.concatenate([self_ref[newest[0]], neigh_ref[newest[0]]], axis=0)
        entered = dot(gather(*newest), enter)
        entered = (entered + bias_ref[newest[0]]).astype(BF16)
        for at, (d, z) in enumerate(tiles):
            enter_ref[z * NY : (z + 1) * NY, d * HID : (d + 1) * HID] = entered[at * NY : (at + 1) * NY]
        outside = jnp.logical_and(at_right, third[1] + 1 == 2 * BLOCK)
        slot = (third[0] + 1) % 2
        for d, z in tiles:
            row = third[1] if d == 0 else jnp.where(outside, SPARE, third[1] + 1)
            normalize(third[0] + 1, hidden_ref[third[1] + d, z], norm_ref.at[slot, row, z])
        for d, z in tiles:
            hidden_ref[second[1] + d, z] += moved[z * NY : (z + 1) * NY, d * HID : (d + 1) * HID]
        layer, x = newest
        ends = x + 2 >= rows_of(layer)[1]
        next_layer = jnp.where(ends, layer + 1, layer)
        next_x = jnp.where(ends, rows_of(layer + 1)[0], x + 2)
        done = next_layer >= LAYERS
        following = (jnp.where(done, 0, next_layer), jnp.where(done, SPARE, next_x))
        return following, newest, second

    def count(layer):
        low, high = rows_of(layer)
        return (high - low + 1) // 2

    total = sum(count(layer) for layer in range(LAYERS))
    none = (jnp.int32(0), jnp.int32(SPARE))
    start = (jnp.int32(0), rows_of(0)[0])
    lax.fori_loop(0, total + 2, turn, (start, none, none))

    found = []
    for z in range(NZ):
        both = jnp.zeros((CHAN * BLOCK, NY), F32)
        for x in range(0, BLOCK, 2):
            pair = jnp.concatenate(
                [norm_ref[0, BLOCK + x + d, z, GROUP : GROUP + NY, :] for d in range(2)], axis=-1
            )
            both = both + dot_nt(dec_ref[x // 2], pair)
        found.append(both)
    change = dot(jnp.concatenate(found, axis=0), grouped(F32), precision=lax.Precision.HIGHEST)
    for c in range(CHAN):
        for z in range(NZ):
            at = (z * CHAN + c) * BLOCK
            state_ref[c, z] = own_ref[c, z] + change[at : at + BLOCK]
    send_ref[...] = state_ref[...].reshape(CHAN * NZ * BLOCK, NY).astype(BF16)


def run_fine_step(*args):
    vmem = pl.BlockSpec(memory_space=pltpu.VMEM)
    return pl.pallas_call(
        fine_step,
        out_shape=(
            jax.ShapeDtypeStruct((CHAN, NZ, BLOCK, NY), F32),
            jax.ShapeDtypeStruct((CHAN * NZ * BLOCK, NY), BF16),
        ),
        in_specs=[pl.BlockSpec(memory_space=pltpu.SMEM)] + [vmem] * 13,
        out_specs=(vmem, vmem),
        scratch_shapes=[
            pltpu.VMEM((HELD, NZ, NY, HID), F32),
            pltpu.VMEM((2, HELD, NZ, PADDED, HID), BF16),
            pltpu.VMEM((NZ * NY, 2 * HID), BF16),
        ],
        compiler_params=pltpu.CompilerParams(vmem_limit_bytes=40 * 2**20),
        cost_estimate=pl.CostEstimate(flops=10**10, bytes_accessed=2**21, transcendentals=10**7),
        name="fine_step",
    )(*args)


def centred(rows):
    return rows - jnp.mean(rows, axis=-1, keepdims=True)


def halves(value):
    high = value.astype(BF16)
    return high, (value - high.astype(F32)).astype(BF16)


def twice(block, none):
    upper = jnp.concatenate([block, none], axis=1)
    return jnp.concatenate([upper, jnp.concatenate([none, block], axis=1)], axis=0)


def prepare(
    plan_ref, rate_ref,
    enc_hbm, type_hbm, force_hbm, gain_hbm, out_hbm, bias_hbm, dec_gain_hbm, dec_hbm,
    enc_first_ref, enc_second_ref, leave_ref, bias_ref, gains_ref, dec_out_ref,
    enc, kind, force, gain, out, bias, dec_gain, dec, sems,
):
    sources = (enc_hbm, type_hbm, force_hbm, gain_hbm, out_hbm, bias_hbm, dec_gain_hbm, dec_hbm)
    targets = (enc, kind, force, gain, out, bias, dec_gain, dec)
    copies = [pltpu.make_async_copy(a, b, sems.at[n]) for n, (a, b) in enumerate(zip(sources, targets))]
    for copy in copies:
        copy.start()
    for copy in copies:
        copy.wait()

    line = lax.broadcasted_iota(jnp.int32, (BLOCK, HID), 0)

    def spread(rows, x):
        return [jnp.where(line == x, row, 0.0) for row in rows]

    weights = halves(centred(enc[...]))
    for step, enc_ref in enumerate((enc_first_ref, enc_second_ref)):
        rate = rate_ref[plan_ref[0, step]]
        push = rate * force[...]
        table = kind[...]
        kinds = halves(centred(jnp.concatenate([table[0:1], table[1:2] + push, table[2:3] - push], axis=0)))
        high, low = [half.astype(F32) for half in weights]
        rows = [part[c : c + 1] for part in (high, low) for c in range(CHAN)]
        rows += [part.astype(F32)[k : k + 1] for part in kinds for k in range(TYPES)]
        for x in range(BLOCK):
            enc_ref[:, x * HID : (x + 1) * HID] = jnp.concatenate(spread(rows, x), axis=0).astype(BF16)
    for layer in range(LAYERS):
        none = jnp.zeros((HID, HID), BF16)
        high, low = halves(centred(out[layer].astype(F32)))
        leave_ref[layer] = jnp.concatenate([twice(high, none), twice(low, none)], axis=0)
        bias_ref[layer] = bias[layer : layer + 1, :] * 0.5
        gains_ref[layer] = gain[layer : layer + 1, :] * (0.5 * HID**0.5)
    gains_ref[LAYERS] = dec_gain[...] * HID**0.5
    rows = [dec[...].astype(F32)[c : c + 1] for c in range(CHAN)]
    for x in range(BLOCK):
        part = jnp.concatenate(spread(rows, x), axis=0).astype(BF16)
        dec_out_ref[x // 2, :, (x % 2) * HID : (x % 2 + 1) * HID] = part


def run_prepare(plan, rate_values, *arrays):
    vmem = pl.BlockSpec(memory_space=pltpu.VMEM)
    smem = pl.BlockSpec(memory_space=pltpu.SMEM)
    shapes = (
        ((FEATURES * BLOCK, BLOCK * HID), BF16),
        ((FEATURES * BLOCK, BLOCK * HID), BF16),
        ((LAYERS, 4 * HID, 2 * HID), BF16),
        ((LAYERS, 1, HID), F32),
        ((LAYERS + 1, 1, HID), F32),
        ((BLOCK // 2, CHAN * BLOCK, 2 * HID), BF16),
    )
    return pl.pallas_call(
        prepare,
        out_shape=tuple(jax.ShapeDtypeStruct(shape, dtype) for shape, dtype in shapes),
        in_specs=[smem] * 2 + [pl.BlockSpec(memory_space=pltpu.HBM)] * len(arrays),
        out_specs=(vmem,) * len(shapes),
        scratch_shapes=[pltpu.VMEM(array.shape, array.dtype) for array in arrays]
        + [pltpu.SemaphoreType.DMA((len(arrays),))],
        compiler_params=pltpu.CompilerParams(vmem_limit_bytes=16 * 2**20),
        cost_estimate=pl.CostEstimate(flops=10**8, bytes_accessed=2**21, transcendentals=0),
        name="prepare",
    )(plan, rate_values, *arrays)


def exchange(value):
    count = lax.axis_size("space")
    first = [(i, i ^ 1) for i in range(count)]
    second = [(i, i + 1) for i in range(1, count - 1, 2)] + [(i + 1, i) for i in range(1, count - 1, 2)]
    return lax.ppermute(value, "space", first), lax.ppermute(value, "space", second)


def matvec(matrix, vector):
    return jnp.sum(matrix * vector[None], axis=1)


def matmat(left, right):
    return jnp.sum(left[:, :, None] * right[None], axis=1)


def per_device(
    prev_starts, plan, cell_type, coarse_matrix, rate_values, enc_weight, type_table, force_vector,
    norm_gain, self_weight, neigh_weight, out_weight, layer_bias, dec_gain, dec_weight,
):
    own = prev_starts[0]
    position = lax.axis_index("space")
    where = jnp.stack([position, lax.axis_size("space") - 1]).astype(jnp.int32)

    outgoing = jnp.concatenate(
        [own.reshape(ROWS, NY), cell_type.astype(F32).reshape(NZ * BLOCK, NY)], axis=0
    ).astype(BF16)
    kinds = sides = exchange(outgoing)
    enc_first, enc_second, *weights = run_prepare(
        plan, rate_values, enc_weight, type_table, force_vector[None], norm_gain,
        out_weight, layer_bias, dec_gain[None], dec_weight,
    )

    state = own
    for step_index in range(STEPS):
        state, outgoing = run_fine_step(
            where, state, *sides, cell_type, *kinds, (enc_first, enc_second)[step_index],
            self_weight, neigh_weight, *weights,
        )
        if step_index + 1 < STEPS:
            sides = exchange(outgoing)

    window = lax.axis_index("tm")
    total = jnp.where(window == 0, state, state - matvec(coarse_matrix, own))
    corrected = total
    power, reach = coarse_matrix, coarse_matrix
    count = lax.axis_size("tm")
    distance = 1
    while distance < count:
        partners = [(i, i ^ SWAPS[distance]) for i in range(count)]
        came = lax.ppermute(total.astype(jnp.float16), "tm", partners).astype(F32)
        upper = (window // distance) % 2 == 1
        corrected = corrected + jnp.where(upper, matvec(reach, came), 0.0)
        if 2 * distance < count:
            lower_total = jnp.where(upper, came, total)
            upper_total = jnp.where(upper, total, came)
            total = upper_total + matvec(power, lower_total)
            reach = jnp.where(upper, matmat(power, reach), reach)
            power = matmat(power, power)
        distance *= 2
    return corrected[None]


def solution(mesh):
    return jax.shard_map(
        per_device,
        mesh=mesh,
        in_specs=(
            P("tm", None, None, "space", None),
            P("tm", None),
            P(None, "space", None),
            P(None, None, None, "space", None),
        )
        + (P(),) * 11,
        out_specs=P("tm", None, None, "space", None),
        check_vma=False,
    )
```

```python
import functools

import jax
import jax.numpy as jnp
from jax import lax
from jax.experimental import pallas as pl
from jax.experimental.pallas import tpu as pltpu
from jax.sharding import PartitionSpec as P

HID = 128
CHAN = 4
NZ = 4
TYPES = 3
RATES = 8
LAYERS = 6
STEPS = 2
NY = 128

EPS = 1e-05

GROUPS, GROUP = 8, 16
PADDED = (GROUPS + 2) * GROUP
BLOCK = 8
FRAME = 3 * BLOCK
SPARE = FRAME + 2
HELD = SPARE + 3
FEATURES = 2 * CHAN + 2 * TYPES
ROWS = CHAN * NZ * BLOCK

SWAPS = {1: 1, 2: 2, 4: 6, 8: 8, 16: 24}

F32, BF16 = jnp.float32, jnp.bfloat16


def dot(a, b, **kw):
    return jnp.dot(a, b, preferred_element_type=F32, **kw)


def dot_nt(a, b):
    return lax.dot_general(a, b, (((1,), (1,)), ((), ())), preferred_element_type=F32)


def twice(block):
    none = jnp.zeros_like(block)
    upper = jnp.concatenate([block, none], axis=1)
    return jnp.concatenate([upper, jnp.concatenate([none, block], axis=1)], axis=0)


def grouped(dtype):
    row = lax.broadcasted_iota(jnp.int32, (NY, NY), 0)
    cell = lax.broadcasted_iota(jnp.int32, (NY, NY), 1)
    return (cell == (row % GROUP) * GROUPS + row // GROUP).astype(dtype)


def fine_step(
    where_ref, own_ref, first_ref, second_ref, kind_ref, kind_first_ref, kind_second_ref,
    enc_ref, self_ref, neigh_ref, out_ref, bias_ref, gain_ref, dec_ref,
    state_ref, send_ref,
    hidden_ref, norm_ref, enter_ref,
):
    order = grouped(F32).astype(BF16)
    position = where_ref[0]
    last = where_ref[1]
    odd = position % 2 == 1
    at_left = position == 0
    at_right = position == last

    def strength(hidden):
        return jnp.sum(hidden * hidden, axis=-1, keepdims=True)

    def normalize(layer, hidden, target):
        normal = hidden * lax.rsqrt(strength(hidden) + HID * EPS) * gain_ref[layer]
        line = lax.broadcasted_iota(jnp.int32, (GROUP, HID), 0)
        before = jnp.where(line == 0, 0.0, pltpu.roll(normal[NY - GROUP :], 1, 0))
        after = jnp.where(line == GROUP - 1, 0.0, pltpu.roll(normal[:GROUP], GROUP - 1, 0))
        target[:GROUP, :] = before.astype(BF16)
        target[GROUP : GROUP + NY, :] = normal.astype(BF16)
        target[GROUP + NY :, :] = after.astype(BF16)

    @pl.when(at_left)
    def _():
        norm_ref[:, BLOCK - 1] = jnp.zeros((2, NZ, PADDED, HID), BF16)

    @pl.when(at_right)
    def _():
        norm_ref[:, 2 * BLOCK] = jnp.zeros((2, NZ, PADDED, HID), BF16)

    def encode(block, states, kinds, xs):
        turned = []
        for z in range(NZ):
            rows = [states[(c * NZ + z) * BLOCK : (c * NZ + z + 1) * BLOCK] for c in range(CHAN)]
            kind_row = kinds[z * BLOCK : (z + 1) * BLOCK]
            marks = [(kind_row == float(kind)).astype(F32) for kind in range(TYPES)]
            table = jnp.concatenate(rows + rows + marks + marks, axis=0).astype(BF16)
            turned.append(dot_nt(order, table).astype(BF16))
        turned = jnp.concatenate(turned, axis=0)
        for first in range(xs.start, xs.stop, 2):
            found = dot(turned, enc_ref[:, first * HID : (first + 2) * HID])
            for x in (first, first + 1):
                for z in range(NZ):
                    hidden = found[z * NY : (z + 1) * NY, (x - first) * HID : (x - first + 1) * HID]
                    hidden_ref[block * BLOCK + x, z] = hidden
                    normalize(0, hidden, norm_ref.at[0, block * BLOCK + x, z])

    encode(1, own_ref[...].reshape(ROWS, NY), kind_ref[...].reshape(NZ * BLOCK, NY).astype(F32), range(BLOCK))

    def neighbour(block, take_first, xs):
        states = jnp.where(take_first, first_ref[:ROWS, :], second_ref[:ROWS, :]).astype(F32)
        kinds = jnp.where(take_first, kind_first_ref[ROWS:, :], kind_second_ref[ROWS:, :]).astype(F32)
        encode(block, states, kinds, xs)

    @pl.when(jnp.logical_not(at_left))
    def _():
        neighbour(0, odd, range(BLOCK - LAYERS, BLOCK))

    @pl.when(jnp.logical_not(at_right))
    def _():
        neighbour(2, jnp.logical_not(odd), range(LAYERS))

    def rows_of(layer):
        reach = LAYERS - 1 - layer
        low = jnp.where(at_left, BLOCK, BLOCK - reach)
        high = jnp.where(at_right, 2 * BLOCK, 2 * BLOCK + reach)
        return low, high

    tiles = [(d, z) for d in range(2) for z in range(NZ)]

    def group(start):
        return slice(start * GROUP, (start + 1) * GROUP)

    def gather(layer, x):
        slot = layer % 2
        loaded = {}

        def read(dx, z, start, own=None):
            loaded_key = (dx, z, start, own)
            if loaded_key not in loaded:
                loaded[loaded_key] = norm_ref[slot, x + dx, z, group(start), :]
            return loaded[loaded_key]

        rows = []
        for d, z in tiles:
            for start in range(1, GROUPS + 1):
                key = (d, z)
                mid = read(d, z, start, key)
                along_x = read(d - 1, z, start, (key, 1)) + read(d + 1, z, start, (key, 1))
                along_y = read(d, z, start - 1, key) + read(d, z, start + 1, key)
                beside = [read(d, w, start, (key, 2)) for w in (z - 1, z + 1) if 0 <= w < NZ]
                along_z = functools.reduce(lambda a, b: a + b, beside)
                rows.append(jnp.concatenate([mid, along_x + along_y + along_z], axis=-1))
        return jnp.concatenate(rows, axis=0)

    def turn(_, pairs):
        newest, second, third = pairs
        half = enter_ref[...]
        message = half * jnp.tanh(half) + half
        leave = jnp.concatenate(
            [twice(out_ref[second[0], :HID]), twice(out_ref[second[0], HID:])], axis=0
        )
        moved = dot(jnp.concatenate([message, message], axis=-1), leave)
        enter = jnp.concatenate([self_ref[newest[0]], neigh_ref[newest[0]]], axis=0)
        entered = dot(gather(*newest), enter)
        entered = (entered + bias_ref[newest[0]]).astype(BF16)
        for at, (d, z) in enumerate(tiles):
            enter_ref[z * NY : (z + 1) * NY, d * HID : (d + 1) * HID] = entered[at * NY : (at + 1) * NY]
        outside = jnp.logical_and(at_right, third[1] + 1 == 2 * BLOCK)
        slot = (third[0] + 1) % 2
        for d, z in tiles:
            row = third[1] if d == 0 else jnp.where(outside, SPARE, third[1] + 1)
            normalize(third[0] + 1, hidden_ref[third[1] + d, z], norm_ref.at[slot, row, z])
        for d, z in tiles:
            hidden_ref[second[1] + d, z] += moved[z * NY : (z + 1) * NY, d * HID : (d + 1) * HID]
        layer, x = newest
        ends = x + 2 >= rows_of(layer)[1]
        next_layer = jnp.where(ends, layer + 1, layer)
        next_x = jnp.where(ends, rows_of(layer + 1)[0], x + 2)
        done = next_layer >= LAYERS
        following = (jnp.where(done, 0, next_layer), jnp.where(done, SPARE, next_x))
        return following, newest, second

    def count(layer):
        low, high = rows_of(layer)
        return (high - low + 1) // 2

    total = sum(count(layer) for layer in range(LAYERS))
    none = (jnp.int32(0), jnp.int32(SPARE))
    start = (jnp.int32(0), rows_of(0)[0])
    lax.fori_loop(0, total + 2, turn, (start, none, none))

    found = []
    for z in range(NZ):
        both = jnp.zeros((CHAN * BLOCK, NY), F32)
        for x in range(0, BLOCK, 2):
            pair = jnp.concatenate(
                [norm_ref[0, BLOCK + x + d, z, GROUP : GROUP + NY, :] for d in range(2)], axis=-1
            )
            both = both + dot_nt(dec_ref[x // 2], pair)
        found.append(both)
    change = dot(jnp.concatenate(found, axis=0), grouped(F32), precision=lax.Precision.HIGHEST)
    for c in range(CHAN):
        for z in range(NZ):
            at = (z * CHAN + c) * BLOCK
            state_ref[c, z] = own_ref[c, z] + change[at : at + BLOCK]
    send_ref[...] = state_ref[...].reshape(CHAN * NZ * BLOCK, NY).astype(BF16)


def run_fine_step(*args):
    vmem = pl.BlockSpec(memory_space=pltpu.VMEM)
    return pl.pallas_call(
        fine_step,
        out_shape=(
            jax.ShapeDtypeStruct((CHAN, NZ, BLOCK, NY), F32),
            jax.ShapeDtypeStruct((CHAN * NZ * BLOCK, NY), BF16),
        ),
        in_specs=[pl.BlockSpec(memory_space=pltpu.SMEM)] + [vmem] * 13,
        out_specs=(vmem, vmem),
        scratch_shapes=[
            pltpu.VMEM((HELD, NZ, NY, HID), F32),
            pltpu.VMEM((2, HELD, NZ, PADDED, HID), BF16),
            pltpu.VMEM((NZ * NY, 2 * HID), BF16),
        ],
        compiler_params=pltpu.CompilerParams(vmem_limit_bytes=26 * 2**20),
        cost_estimate=pl.CostEstimate(flops=10**10, bytes_accessed=2**21, transcendentals=10**7),
        name="fine_step",
    )(*args)


def centred(rows):
    return rows - jnp.mean(rows, axis=-1, keepdims=True)


def halves(value):
    high = value.astype(BF16)
    return high, (value - high.astype(F32)).astype(BF16)


def prepare(
    plan_ref, rate_ref,
    enc_hbm, type_hbm, force_hbm, gain_hbm, out_hbm, bias_hbm, dec_gain_hbm, dec_hbm,
    enc_first_ref, enc_second_ref, leave_ref, bias_ref, gains_ref, dec_out_ref,
    enc, kind, force, gain, out, bias, dec_gain, dec, sems,
):
    sources = (enc_hbm, type_hbm, force_hbm, gain_hbm, out_hbm, bias_hbm, dec_gain_hbm, dec_hbm)
    targets = (enc, kind, force, gain, out, bias, dec_gain, dec)
    copies = [pltpu.make_async_copy(a, b, sems.at[n]) for n, (a, b) in enumerate(zip(sources, targets))]
    for copy in copies:
        copy.start()
    for copy in copies:
        copy.wait()

    line = lax.broadcasted_iota(jnp.int32, (BLOCK, HID), 0)

    def spread(rows, x):
        return [jnp.where(line == x, row, 0.0) for row in rows]

    weights = halves(centred(enc[...]))
    for step, enc_ref in enumerate((enc_first_ref, enc_second_ref)):
        rate = rate_ref[plan_ref[0, step]]
        push = rate * force[...]
        table = kind[...]
        kinds = halves(centred(jnp.concatenate([table[0:1], table[1:2] + push, table[2:3] - push], axis=0)))
        high, low = [half.astype(F32) for half in weights]
        rows = [part[c : c + 1] for part in (high, low) for c in range(CHAN)]
        rows += [part.astype(F32)[k : k + 1] for part in kinds for k in range(TYPES)]
        for x in range(BLOCK):
            enc_ref[:, x * HID : (x + 1) * HID] = jnp.concatenate(spread(rows, x), axis=0).astype(BF16)
    for layer in range(LAYERS):
        high, low = halves(centred(out[layer].astype(F32)))
        leave_ref[layer, :HID, :] = high
        leave_ref[layer, HID:, :] = low
        bias_ref[layer] = bias[layer : layer + 1, :] * 0.5
        gains_ref[layer] = gain[layer : layer + 1, :] * (0.5 * HID**0.5)
    gains_ref[LAYERS] = dec_gain[...] * HID**0.5
    rows = [dec[...].astype(F32)[c : c + 1] for c in range(CHAN)]
    for x in range(BLOCK):
        part = jnp.concatenate(spread(rows, x), axis=0).astype(BF16)
        dec_out_ref[x // 2, :, (x % 2) * HID : (x % 2 + 1) * HID] = part


def run_prepare(plan, rate_values, *arrays):
    vmem = pl.BlockSpec(memory_space=pltpu.VMEM)
    smem = pl.BlockSpec(memory_space=pltpu.SMEM)
    shapes = (
        ((FEATURES * BLOCK, BLOCK * HID), BF16),
        ((FEATURES * BLOCK, BLOCK * HID), BF16),
        ((LAYERS, 2 * HID, HID), BF16),
        ((LAYERS, 1, HID), F32),
        ((LAYERS + 1, 1, HID), F32),
        ((BLOCK // 2, CHAN * BLOCK, 2 * HID), BF16),
    )
    return pl.pallas_call(
        prepare,
        out_shape=tuple(jax.ShapeDtypeStruct(shape, dtype) for shape, dtype in shapes),
        in_specs=[smem] * 2 + [pl.BlockSpec(memory_space=pltpu.HBM)] * len(arrays),
        out_specs=(vmem,) * len(shapes),
        scratch_shapes=[pltpu.VMEM(array.shape, array.dtype) for array in arrays]
        + [pltpu.SemaphoreType.DMA((len(arrays),))],
        compiler_params=pltpu.CompilerParams(vmem_limit_bytes=8 * 2**20),
        cost_estimate=pl.CostEstimate(flops=10**8, bytes_accessed=2**21, transcendentals=0),
        name="prepare",
    )(plan, rate_values, *arrays)


def exchange(value):
    count = lax.axis_size("space")
    first = [(i, i ^ 1) for i in range(count)]
    second = [(i, i + 1) for i in range(1, count - 1, 2)] + [(i + 1, i) for i in range(1, count - 1, 2)]
    return lax.ppermute(value, "space", first), lax.ppermute(value, "space", second)


def matvec(matrix, vector):
    return jnp.sum(matrix * vector[None], axis=1)


def matmat(left, right):
    return jnp.sum(left[:, :, None] * right[None], axis=1)


def per_device(
    prev_starts, plan, cell_type, coarse_matrix, rate_values, enc_weight, type_table, force_vector,
    norm_gain, self_weight, neigh_weight, out_weight, layer_bias, dec_gain, dec_weight,
):
    own = prev_starts[0]
    position = lax.axis_index("space")
    where = jnp.stack([position, lax.axis_size("space") - 1]).astype(jnp.int32)

    outgoing = jnp.concatenate(
        [own.reshape(ROWS, NY), cell_type.astype(F32).reshape(NZ * BLOCK, NY)], axis=0
    ).astype(BF16)
    kinds = sides = exchange(outgoing)
    enc_first, enc_second, *weights = run_prepare(
        plan, rate_values, enc_weight, type_table, force_vector[None], norm_gain,
        out_weight, layer_bias, dec_gain[None], dec_weight,
    )

    state = own
    for step_index in range(STEPS):
        state, outgoing = run_fine_step(
            where, state, *sides, cell_type, *kinds, (enc_first, enc_second)[step_index],
            self_weight, neigh_weight, *weights,
        )
        if step_index + 1 < STEPS:
            sides = exchange(outgoing)

    window = lax.axis_index("tm")
    total = jnp.where(window == 0, state, state - matvec(coarse_matrix, own))
    corrected = total
    power, reach = coarse_matrix, coarse_matrix
    count = lax.axis_size("tm")
    distance = 1
    while distance < count:
        partners = [(i, i ^ SWAPS[distance]) for i in range(count)]
        came = lax.ppermute(total.astype(jnp.float16), "tm", partners).astype(F32)
        upper = (window // distance) % 2 == 1
        corrected = corrected + jnp.where(upper, matvec(reach, came), 0.0)
        if 2 * distance < count:
            lower_total = jnp.where(upper, came, total)
            upper_total = jnp.where(upper, total, came)
            total = upper_total + matvec(power, lower_total)
            reach = jnp.where(upper, matmat(power, reach), reach)
            power = matmat(power, power)
        distance *= 2
    return corrected[None]


def solution(mesh):
    return jax.shard_map(
        per_device,
        mesh=mesh,
        in_specs=(
            P("tm", None, None, "space", None),
            P("tm", None),
            P(None, "space", None),
            P(None, None, None, "space", None),
        )
        + (P(),) * 11,
        out_specs=P("tm", None, None, "space", None),
        check_vma=False,
    )
```

```python
import functools

import jax
import jax.numpy as jnp
from jax import lax
from jax.experimental import pallas as pl
from jax.experimental.pallas import tpu as pltpu
from jax.sharding import PartitionSpec as P

HID = 128
CHAN = 4
NZ = 4
TYPES = 3
RATES = 8
LAYERS = 6
STEPS = 2
NY = 128

EPS = 1e-05

GROUPS, GROUP = 8, 16
PADDED = (GROUPS + 2) * GROUP
BLOCK = 8
FRAME = 3 * BLOCK
SPARE = FRAME + 2
HELD = SPARE + 3
FEATURES = 2 * CHAN + 2 * TYPES
ROWS = CHAN * NZ * BLOCK

SWAPS = {1: 1, 2: 2, 4: 6, 8: 8, 16: 24}

F32, BF16 = jnp.float32, jnp.bfloat16


def dot(a, b, **kw):
    return jnp.dot(a, b, preferred_element_type=F32, **kw)


def dot_nt(a, b):
    return lax.dot_general(a, b, (((1,), (1,)), ((), ())), preferred_element_type=F32)


def twice(block):
    none = jnp.zeros_like(block)
    upper = jnp.concatenate([block, none], axis=1)
    return jnp.concatenate([upper, jnp.concatenate([none, block], axis=1)], axis=0)


def grouped(dtype):
    row = lax.broadcasted_iota(jnp.int32, (NY, NY), 0)
    cell = lax.broadcasted_iota(jnp.int32, (NY, NY), 1)
    return (cell == (row % GROUP) * GROUPS + row // GROUP).astype(dtype)


def fine_step(
    where_ref, own_ref, first_ref, second_ref, kind_ref, kind_first_ref, kind_second_ref,
    enc_ref, self_ref, neigh_ref, out_ref, bias_ref, gain_ref, dec_ref,
    state_ref, send_ref,
    hidden_ref, norm_ref, enter_ref,
):
    order = grouped(F32).astype(BF16)
    position = where_ref[0]
    last = where_ref[1]
    odd = position % 2 == 1
    at_left = position == 0
    at_right = position == last

    def strength(hidden):
        return jnp.sum(hidden * hidden, axis=-1, keepdims=True)

    def normalize(layer, hidden, target):
        normal = hidden * lax.rsqrt(strength(hidden) + HID * EPS) * gain_ref[layer]
        line = lax.broadcasted_iota(jnp.int32, (GROUP, HID), 0)
        before = jnp.where(line == 0, 0.0, pltpu.roll(normal[NY - GROUP :], 1, 0))
        after = jnp.where(line == GROUP - 1, 0.0, pltpu.roll(normal[:GROUP], GROUP - 1, 0))
        target[:GROUP, :] = before.astype(BF16)
        target[GROUP : GROUP + NY, :] = normal.astype(BF16)
        target[GROUP + NY :, :] = after.astype(BF16)

    @pl.when(at_left)
    def _():
        norm_ref[:, BLOCK - 1] = jnp.zeros((2, NZ, PADDED, HID), BF16)

    @pl.when(at_right)
    def _():
        norm_ref[:, 2 * BLOCK] = jnp.zeros((2, NZ, PADDED, HID), BF16)

    def encode(block, states, kinds, xs):
        turned = []
        for z in range(NZ):
            rows = [states[(c * NZ + z) * BLOCK : (c * NZ + z + 1) * BLOCK] for c in range(CHAN)]
            kind_row = kinds[z * BLOCK : (z + 1) * BLOCK]
            marks = [(kind_row == float(kind)).astype(F32) for kind in range(TYPES)]
            table = jnp.concatenate(rows + rows + marks + marks, axis=0).astype(BF16)
            turned.append(dot_nt(order, table).astype(BF16))
        turned = jnp.concatenate(turned, axis=0)
        for first in range(xs.start, xs.stop, 2):
            found = dot(turned, enc_ref[:, first * HID : (first + 2) * HID])
            for x in (first, first + 1):
                for z in range(NZ):
                    hidden = found[z * NY : (z + 1) * NY, (x - first) * HID : (x - first + 1) * HID]
                    hidden_ref[block * BLOCK + x, z] = hidden
                    normalize(0, hidden, norm_ref.at[0, block * BLOCK + x, z])

    encode(1, own_ref[...].reshape(ROWS, NY), kind_ref[...].reshape(NZ * BLOCK, NY).astype(F32), range(BLOCK))

    def neighbour(block, take_first, xs):
        states = jnp.where(take_first, first_ref[:ROWS, :], second_ref[:ROWS, :]).astype(F32)
        kinds = jnp.where(take_first, kind_first_ref[ROWS:, :], kind_second_ref[ROWS:, :]).astype(F32)
        encode(block, states, kinds, xs)

    @pl.when(jnp.logical_not(at_left))
    def _():
        neighbour(0, odd, range(BLOCK - LAYERS, BLOCK))

    @pl.when(jnp.logical_not(at_right))
    def _():
        neighbour(2, jnp.logical_not(odd), range(LAYERS))

    def rows_of(layer):
        reach = LAYERS - 1 - layer
        low = jnp.where(at_left, BLOCK, BLOCK - reach)
        high = jnp.where(at_right, 2 * BLOCK, 2 * BLOCK + reach)
        return low, high

    tiles = [(d, z) for d in range(2) for z in range(NZ)]

    def group(start):
        return slice(start * GROUP, (start + 1) * GROUP)

    def gather(layer, x):
        slot = layer % 2
        loaded = {}

        def read(dx, z, start, own=None):
            loaded_key = (dx, z, start, own)
            if loaded_key not in loaded:
                loaded[loaded_key] = norm_ref[slot, x + dx, z, group(start), :]
            return loaded[loaded_key]

        rows = []
        for d, z in tiles:
            for start in range(1, GROUPS + 1):
                key = (d, z)
                mid = read(d, z, start, key)
                along_x = read(d - 1, z, start, (key, 1)) + read(d + 1, z, start, (key, 1))
                along_y = read(d, z, start - 1, key) + read(d, z, start + 1, key)
                beside = [read(d, w, start, (key, 2)) for w in (z - 1, z + 1) if 0 <= w < NZ]
                along_z = functools.reduce(lambda a, b: a + b, beside)
                rows.append(jnp.concatenate([mid, along_x + along_y + along_z], axis=-1))
        return jnp.concatenate(rows, axis=0)

    def turn(_, pairs):
        newest, second, third = pairs
        half = enter_ref[...]
        message = half * jnp.tanh(half) + half
        leave = jnp.concatenate(
            [twice(out_ref[second[0], :HID]), twice(out_ref[second[0], HID:])], axis=0
        )
        moved = dot(jnp.concatenate([message, message], axis=-1), leave)
        enter = jnp.concatenate([self_ref[newest[0]], neigh_ref[newest[0]]], axis=0)
        entered = dot(gather(*newest), enter)
        entered = (entered + bias_ref[newest[0]]).astype(BF16)
        for at, (d, z) in enumerate(tiles):
            enter_ref[z * NY : (z + 1) * NY, d * HID : (d + 1) * HID] = entered[at * NY : (at + 1) * NY]
        outside = jnp.logical_and(at_right, third[1] + 1 == 2 * BLOCK)
        slot = (third[0] + 1) % 2
        for d, z in tiles:
            row = third[1] if d == 0 else jnp.where(outside, SPARE, third[1] + 1)
            normalize(third[0] + 1, hidden_ref[third[1] + d, z], norm_ref.at[slot, row, z])
        for d, z in tiles:
            hidden_ref[second[1] + d, z] += moved[z * NY : (z + 1) * NY, d * HID : (d + 1) * HID]
        layer, x = newest
        ends = x + 2 >= rows_of(layer)[1]
        next_layer = jnp.where(ends, layer + 1, layer)
        next_x = jnp.where(ends, rows_of(layer + 1)[0], x + 2)
        done = next_layer >= LAYERS
        following = (jnp.where(done, 0, next_layer), jnp.where(done, SPARE, next_x))
        return following, newest, second

    def count(layer):
        low, high = rows_of(layer)
        return (high - low + 1) // 2

    total = sum(count(layer) for layer in range(LAYERS))
    none = (jnp.int32(0), jnp.int32(SPARE))
    start = (jnp.int32(0), rows_of(0)[0])
    lax.fori_loop(0, total + 2, turn, (start, none, none))

    found = []
    for z in range(NZ):
        both = jnp.zeros((CHAN * BLOCK, NY), F32)
        for x in range(0, BLOCK, 2):
            pair = jnp.concatenate(
                [norm_ref[0, BLOCK + x + d, z, GROUP : GROUP + NY, :] for d in range(2)], axis=-1
            )
            both = both + dot_nt(dec_ref[x // 2], pair)
        found.append(both)
    change = dot(jnp.concatenate(found, axis=0), grouped(F32), precision=lax.Precision.HIGHEST)
    for c in range(CHAN):
        for z in range(NZ):
            at = (z * CHAN + c) * BLOCK
            state_ref[c, z] = own_ref[c, z] + change[at : at + BLOCK]
    send_ref[...] = state_ref[...].reshape(CHAN * NZ * BLOCK, NY).astype(BF16)


def run_fine_step(*args):
    vmem = pl.BlockSpec(memory_space=pltpu.VMEM)
    return pl.pallas_call(
        fine_step,
        out_shape=(
            jax.ShapeDtypeStruct((CHAN, NZ, BLOCK, NY), F32),
            jax.ShapeDtypeStruct((CHAN * NZ * BLOCK, NY), BF16),
        ),
        in_specs=[pl.BlockSpec(memory_space=pltpu.SMEM)] + [vmem] * 13,
        out_specs=(vmem, vmem),
        scratch_shapes=[
            pltpu.VMEM((HELD, NZ, NY, HID), F32),
            pltpu.VMEM((2, HELD, NZ, PADDED, HID), BF16),
            pltpu.VMEM((NZ * NY, 2 * HID), BF16),
        ],
        compiler_params=pltpu.CompilerParams(vmem_limit_bytes=26 * 2**20),
        cost_estimate=pl.CostEstimate(flops=10**10, bytes_accessed=2**21, transcendentals=10**7),
        name="fine_step",
    )(*args)


def centred(rows):
    return rows - jnp.mean(rows, axis=-1, keepdims=True)


def halves(value):
    high = value.astype(BF16)
    return high, (value - high.astype(F32)).astype(BF16)


def prepare(
    plan_ref, rate_ref,
    enc_hbm, type_hbm, force_hbm, gain_hbm, out_hbm, bias_hbm, dec_gain_hbm, dec_hbm, neigh_hbm,
    enc_first_ref, enc_second_ref, neigh_ref, leave_ref, bias_ref, gains_ref, dec_out_ref,
    enc, kind, force, gain, out, bias, dec_gain, dec, sems,
):
    sources = (enc_hbm, type_hbm, force_hbm, gain_hbm, out_hbm, bias_hbm, dec_gain_hbm, dec_hbm, neigh_hbm)
    targets = (enc, kind, force, gain, out, bias, dec_gain, dec, neigh_ref)
    copies = [pltpu.make_async_copy(a, b, sems.at[n]) for n, (a, b) in enumerate(zip(sources, targets))]
    for copy in copies:
        copy.start()
    for copy in copies[:-1]:
        copy.wait()

    line = lax.broadcasted_iota(jnp.int32, (BLOCK, HID), 0)

    def spread(rows, x):
        return [jnp.where(line == x, row, 0.0) for row in rows]

    weights = halves(centred(enc[...]))
    for step, enc_ref in enumerate((enc_first_ref, enc_second_ref)):
        rate = rate_ref[plan_ref[0, step]]
        push = rate * force[...]
        table = kind[...]
        kinds = halves(centred(jnp.concatenate([table[0:1], table[1:2] + push, table[2:3] - push], axis=0)))
        high, low = [half.astype(F32) for half in weights]
        rows = [part[c : c + 1] for part in (high, low) for c in range(CHAN)]
        rows += [part.astype(F32)[k : k + 1] for part in kinds for k in range(TYPES)]
        for x in range(BLOCK):
            enc_ref[:, x * HID : (x + 1) * HID] = jnp.concatenate(spread(rows, x), axis=0).astype(BF16)
    for layer in range(LAYERS):
        high, low = halves(centred(out[layer].astype(F32)))
        leave_ref[layer, :HID, :] = high
        leave_ref[layer, HID:, :] = low
        bias_ref[layer] = bias[layer : layer + 1, :] * 0.5
        gains_ref[layer] = gain[layer : layer + 1, :] * (0.5 * HID**0.5)
    gains_ref[LAYERS] = dec_gain[...] * HID**0.5
    rows = [dec[...].astype(F32)[c : c + 1] for c in range(CHAN)]
    for x in range(BLOCK):
        part = jnp.concatenate(spread(rows, x), axis=0).astype(BF16)
        dec_out_ref[x // 2, :, (x % 2) * HID : (x % 2 + 1) * HID] = part
    copies[-1].wait()


def run_prepare(plan, rate_values, *arrays):
    vmem = pl.BlockSpec(memory_space=pltpu.VMEM)
    smem = pl.BlockSpec(memory_space=pltpu.SMEM)
    shapes = (
        ((FEATURES * BLOCK, BLOCK * HID), BF16),
        ((FEATURES * BLOCK, BLOCK * HID), BF16),
        ((LAYERS, HID, HID), BF16),
        ((LAYERS, 2 * HID, HID), BF16),
        ((LAYERS, 1, HID), F32),
        ((LAYERS + 1, 1, HID), F32),
        ((BLOCK // 2, CHAN * BLOCK, 2 * HID), BF16),
    )
    return pl.pallas_call(
        prepare,
        out_shape=tuple(jax.ShapeDtypeStruct(shape, dtype) for shape, dtype in shapes),
        in_specs=[smem] * 2 + [pl.BlockSpec(memory_space=pltpu.HBM)] * len(arrays),
        out_specs=(vmem,) * len(shapes),
        scratch_shapes=[pltpu.VMEM(array.shape, array.dtype) for array in arrays[:-1]]
        + [pltpu.SemaphoreType.DMA((len(arrays),))],
        compiler_params=pltpu.CompilerParams(vmem_limit_bytes=8 * 2**20),
        cost_estimate=pl.CostEstimate(flops=10**8, bytes_accessed=2**21, transcendentals=0),
        name="prepare",
    )(plan, rate_values, *arrays)


def exchange(value):
    count = lax.axis_size("space")
    first = [(i, i ^ 1) for i in range(count)]
    second = [(i, i + 1) for i in range(1, count - 1, 2)] + [(i + 1, i) for i in range(1, count - 1, 2)]
    return lax.ppermute(value, "space", first), lax.ppermute(value, "space", second)


def matvec(matrix, vector):
    return jnp.sum(matrix * vector[None], axis=1)


def matmat(left, right):
    return jnp.sum(left[:, :, None] * right[None], axis=1)


def per_device(
    prev_starts, plan, cell_type, coarse_matrix, rate_values, enc_weight, type_table, force_vector,
    norm_gain, self_weight, neigh_weight, out_weight, layer_bias, dec_gain, dec_weight,
):
    own = prev_starts[0]
    position = lax.axis_index("space")
    where = jnp.stack([position, lax.axis_size("space") - 1]).astype(jnp.int32)

    outgoing = jnp.concatenate(
        [own.reshape(ROWS, NY), cell_type.astype(F32).reshape(NZ * BLOCK, NY)], axis=0
    ).astype(BF16)
    kinds = sides = exchange(outgoing)
    enc_first, enc_second, *weights = run_prepare(
        plan, rate_values, enc_weight, type_table, force_vector[None], norm_gain,
        out_weight, layer_bias, dec_gain[None], dec_weight, neigh_weight,
    )

    state = own
    for step_index in range(STEPS):
        state, outgoing = run_fine_step(
            where, state, *sides, cell_type, *kinds, (enc_first, enc_second)[step_index],
            self_weight, *weights,
        )
        if step_index + 1 < STEPS:
            sides = exchange(outgoing)

    window = lax.axis_index("tm")
    total = jnp.where(window == 0, state, state - matvec(coarse_matrix, own))
    corrected = total
    power, reach = coarse_matrix, coarse_matrix
    count = lax.axis_size("tm")
    distance = 1
    while distance < count:
        partners = [(i, i ^ SWAPS[distance]) for i in range(count)]
        came = lax.ppermute(total.astype(jnp.float16), "tm", partners).astype(F32)
        upper = (window // distance) % 2 == 1
        corrected = corrected + jnp.where(upper, matvec(reach, came), 0.0)
        if 2 * distance < count:
            lower_total = jnp.where(upper, came, total)
            upper_total = jnp.where(upper, total, came)
            total = upper_total + matvec(power, lower_total)
            reach = jnp.where(upper, matmat(power, reach), reach)
            power = matmat(power, power)
        distance *= 2
    return corrected[None]


def solution(mesh):
    return jax.shard_map(
        per_device,
        mesh=mesh,
        in_specs=(
            P("tm", None, None, "space", None),
            P("tm", None),
            P(None, "space", None),
            P(None, None, None, "space", None),
        )
        + (P(),) * 11,
        out_specs=P("tm", None, None, "space", None),
        check_vma=False,
    )
```

```python
import functools

import jax
import jax.numpy as jnp
from jax import lax
from jax.experimental import pallas as pl
from jax.experimental.pallas import tpu as pltpu
from jax.sharding import PartitionSpec as P

HID = 128
CHAN = 4
NZ = 4
TYPES = 3
RATES = 8
LAYERS = 6
STEPS = 2
NY = 128

EPS = 1e-05

GROUPS, GROUP = 8, 16
PADDED = (GROUPS + 2) * GROUP
BLOCK = 8
FRAME = 3 * BLOCK
SPARE = FRAME + 2
HELD = SPARE + 3
FEATURES = 2 * CHAN + 2 * TYPES
ROWS = CHAN * NZ * BLOCK

SWAPS = {1: 1, 2: 2, 4: 6, 8: 8, 16: 24}

F32, BF16 = jnp.float32, jnp.bfloat16


def dot(a, b, **kw):
    return jnp.dot(a, b, preferred_element_type=F32, **kw)


def dot_nt(a, b):
    return lax.dot_general(a, b, (((1,), (1,)), ((), ())), preferred_element_type=F32)


def twice(block):
    none = jnp.zeros_like(block)
    upper = jnp.concatenate([block, none], axis=1)
    return jnp.concatenate([upper, jnp.concatenate([none, block], axis=1)], axis=0)


def grouped(dtype):
    row = lax.broadcasted_iota(jnp.int32, (NY, NY), 0)
    cell = lax.broadcasted_iota(jnp.int32, (NY, NY), 1)
    return (cell == (row % GROUP) * GROUPS + row // GROUP).astype(dtype)


def fine_step(
    where_ref, own_ref, first_ref, second_ref, kind_ref, kind_first_ref, kind_second_ref,
    enc_ref, self_ref, neigh_ref, out_ref, bias_ref, gain_ref, dec_ref,
    state_ref, send_ref,
    hidden_ref, norm_ref, enter_ref,
):
    order = grouped(F32).astype(BF16)
    position = where_ref[0]
    last = where_ref[1]
    odd = position % 2 == 1
    at_left = position == 0
    at_right = position == last

    def strength(hidden):
        return jnp.sum(hidden * hidden, axis=-1, keepdims=True)

    def normalize(layer, hidden, target):
        normal = hidden * lax.rsqrt(strength(hidden) + HID * EPS) * gain_ref[layer]
        line = lax.broadcasted_iota(jnp.int32, (GROUP, HID), 0)
        before = jnp.where(line == 0, 0.0, pltpu.roll(normal[NY - GROUP :], 1, 0))
        after = jnp.where(line == GROUP - 1, 0.0, pltpu.roll(normal[:GROUP], GROUP - 1, 0))
        target[:GROUP, :] = before.astype(BF16)
        target[GROUP : GROUP + NY, :] = normal.astype(BF16)
        target[GROUP + NY :, :] = after.astype(BF16)

    @pl.when(at_left)
    def _():
        norm_ref[:, BLOCK - 1] = jnp.zeros((2, NZ, PADDED, HID), BF16)

    @pl.when(at_right)
    def _():
        norm_ref[:, 2 * BLOCK] = jnp.zeros((2, NZ, PADDED, HID), BF16)

    def encode(block, states, kinds, xs):
        turned = []
        for z in range(NZ):
            rows = [states[(c * NZ + z) * BLOCK : (c * NZ + z + 1) * BLOCK] for c in range(CHAN)]
            kind_row = kinds[z * BLOCK : (z + 1) * BLOCK]
            marks = [(kind_row == float(kind)).astype(F32) for kind in range(TYPES)]
            table = jnp.concatenate(rows + rows + marks + marks, axis=0).astype(BF16)
            turned.append(dot_nt(order, table).astype(BF16))
        turned = jnp.concatenate(turned, axis=0)
        for first in range(xs.start, xs.stop, 2):
            found = dot(turned, enc_ref[:, first * HID : (first + 2) * HID])
            for x in (first, first + 1):
                for z in range(NZ):
                    hidden = found[z * NY : (z + 1) * NY, (x - first) * HID : (x - first + 1) * HID]
                    hidden_ref[block * BLOCK + x, z] = hidden
                    normalize(0, hidden, norm_ref.at[0, block * BLOCK + x, z])

    encode(1, own_ref[...].reshape(ROWS, NY), kind_ref[...].reshape(NZ * BLOCK, NY).astype(F32), range(BLOCK))

    def neighbour(block, take_first, xs):
        states = jnp.where(take_first, first_ref[:ROWS, :], second_ref[:ROWS, :]).astype(F32)
        kinds = jnp.where(take_first, kind_first_ref[ROWS:, :], kind_second_ref[ROWS:, :]).astype(F32)
        encode(block, states, kinds, xs)

    @pl.when(jnp.logical_not(at_left))
    def _():
        neighbour(0, odd, range(BLOCK - LAYERS, BLOCK))

    @pl.when(jnp.logical_not(at_right))
    def _():
        neighbour(2, jnp.logical_not(odd), range(LAYERS))

    def rows_of(layer):
        reach = LAYERS - 1 - layer
        low = jnp.where(at_left, BLOCK, BLOCK - reach)
        high = jnp.where(at_right, 2 * BLOCK, 2 * BLOCK + reach)
        return low, high

    tiles = [(d, z) for d in range(2) for z in range(NZ)]

    def group(start):
        return slice(start * GROUP, (start + 1) * GROUP)

    def gather(layer, x):
        slot = layer % 2
        loaded = {}

        def read(dx, z, start, own=None):
            loaded_key = (dx, z, start, own)
            if loaded_key not in loaded:
                loaded[loaded_key] = norm_ref[slot, x + dx, z, group(start), :]
            return loaded[loaded_key]

        rows = []
        for d, z in tiles:
            for start in range(1, GROUPS + 1):
                key = (d, z)
                mid = read(d, z, start, key)
                along_x = read(d - 1, z, start, (key, 1)) + read(d + 1, z, start, (key, 1))
                along_y = read(d, z, start - 1, key) + read(d, z, start + 1, key)
                beside = [read(d, w, start, (key, 2)) for w in (z - 1, z + 1) if 0 <= w < NZ]
                along_z = functools.reduce(lambda a, b: a + b, beside)
                rows.append(jnp.concatenate([mid, along_x + along_y + along_z], axis=-1))
        return jnp.concatenate(rows, axis=0)

    def turn(_, pairs):
        newest, second, third = pairs
        half = enter_ref[...]
        message = half * jnp.tanh(half) + half
        leave = jnp.concatenate(
            [twice(out_ref[second[0], :HID]), twice(out_ref[second[0], HID:])], axis=0
        )
        moved = dot(jnp.concatenate([message, message], axis=-1), leave)
        enter = jnp.concatenate([self_ref[newest[0]], neigh_ref[newest[0]]], axis=0)
        entered = dot(gather(*newest), enter)
        entered = (entered + bias_ref[newest[0]]).astype(BF16)
        for at, (d, z) in enumerate(tiles):
            enter_ref[z * NY : (z + 1) * NY, d * HID : (d + 1) * HID] = entered[at * NY : (at + 1) * NY]
        outside = jnp.logical_and(at_right, third[1] + 1 == 2 * BLOCK)
        slot = (third[0] + 1) % 2
        for d, z in tiles:
            row = third[1] if d == 0 else jnp.where(outside, SPARE, third[1] + 1)
            normalize(third[0] + 1, hidden_ref[third[1] + d, z], norm_ref.at[slot, row, z])
        for d, z in tiles:
            hidden_ref[second[1] + d, z] += moved[z * NY : (z + 1) * NY, d * HID : (d + 1) * HID]
        layer, x = newest
        ends = x + 2 >= rows_of(layer)[1]
        next_layer = jnp.where(ends, layer + 1, layer)
        next_x = jnp.where(ends, rows_of(layer + 1)[0], x + 2)
        done = next_layer >= LAYERS
        following = (jnp.where(done, 0, next_layer), jnp.where(done, SPARE, next_x))
        return following, newest, second

    def count(layer):
        low, high = rows_of(layer)
        return (high - low + 1) // 2

    total = sum(count(layer) for layer in range(LAYERS))
    none = (jnp.int32(0), jnp.int32(SPARE))
    start = (jnp.int32(0), rows_of(0)[0])
    lax.fori_loop(0, total + 2, turn, (start, none, none))

    found = []
    for z in range(NZ):
        both = jnp.zeros((CHAN * BLOCK, NY), F32)
        for x in range(0, BLOCK, 2):
            pair = jnp.concatenate(
                [norm_ref[0, BLOCK + x + d, z, GROUP : GROUP + NY, :] for d in range(2)], axis=-1
            )
            both = both + dot_nt(dec_ref[x // 2], pair)
        found.append(both)
    change = dot(jnp.concatenate(found, axis=0), grouped(F32), precision=lax.Precision.HIGHEST)
    for c in range(CHAN):
        for z in range(NZ):
            at = (z * CHAN + c) * BLOCK
            state_ref[c, z] = own_ref[c, z] + change[at : at + BLOCK]
    send_ref[...] = state_ref[...].reshape(CHAN * NZ * BLOCK, NY).astype(BF16)


def run_fine_step(*args):
    vmem = pl.BlockSpec(memory_space=pltpu.VMEM)
    return pl.pallas_call(
        fine_step,
        out_shape=(
            jax.ShapeDtypeStruct((CHAN, NZ, BLOCK, NY), F32),
            jax.ShapeDtypeStruct((CHAN * NZ * BLOCK, NY), BF16),
        ),
        in_specs=[pl.BlockSpec(memory_space=pltpu.SMEM)] + [vmem] * 13,
        out_specs=(vmem, vmem),
        scratch_shapes=[
            pltpu.VMEM((HELD, NZ, NY, HID), F32),
            pltpu.VMEM((2, HELD, NZ, PADDED, HID), BF16),
            pltpu.VMEM((NZ * NY, 2 * HID), BF16),
        ],
        compiler_params=pltpu.CompilerParams(vmem_limit_bytes=26 * 2**20),
        cost_estimate=pl.CostEstimate(flops=10**10, bytes_accessed=2**21, transcendentals=10**7),
        name="fine_step",
    )(*args)


def centred(rows):
    return rows - jnp.mean(rows, axis=-1, keepdims=True)


def halves(value):
    high = value.astype(BF16)
    return high, (value - high.astype(F32)).astype(BF16)


def prepare(
    plan_ref, rate_ref,
    enc_hbm, type_hbm, force_hbm, gain_hbm, out_hbm, bias_hbm, dec_gain_hbm, dec_hbm, neigh_hbm,
    enc_first_ref, enc_second_ref, neigh_ref, leave_ref, bias_ref, gains_ref, dec_out_ref,
    enc, kind, force, gain, out, bias, dec_gain, dec, sems,
):
    sources = (enc_hbm, type_hbm, force_hbm, gain_hbm, out_hbm, bias_hbm, dec_gain_hbm, dec_hbm, neigh_hbm)
    targets = (enc, kind, force, gain, out, bias, dec_gain, dec, neigh_ref)
    copies = [pltpu.make_async_copy(a, b, sems.at[n]) for n, (a, b) in enumerate(zip(sources, targets))]
    for copy in copies:
        copy.start()
    for copy in copies[:-1]:
        copy.wait()

    line = lax.broadcasted_iota(jnp.int32, (BLOCK, HID), 0)

    def spread(rows, x):
        return [jnp.where(line == x, row, 0.0) for row in rows]

    weights = halves(centred(enc[...]))
    for step, enc_ref in enumerate((enc_first_ref, enc_second_ref)):
        rate = rate_ref[plan_ref[0, step]]
        push = rate * force[...]
        table = kind[...]
        kinds = halves(centred(jnp.concatenate([table[0:1], table[1:2] + push, table[2:3] - push], axis=0)))
        high, low = [half.astype(F32) for half in weights]
        rows = [part[c : c + 1] for part in (high, low) for c in range(CHAN)]
        rows += [part.astype(F32)[k : k + 1] for part in kinds for k in range(TYPES)]
        for x in range(BLOCK):
            enc_ref[:, x * HID : (x + 1) * HID] = jnp.concatenate(spread(rows, x), axis=0).astype(BF16)
    for layer in range(LAYERS):
        high, low = halves(centred(out[layer].astype(F32)))
        leave_ref[layer, :HID, :] = high
        leave_ref[layer, HID:, :] = low
        bias_ref[layer] = bias[layer : layer + 1, :] * 0.5
        gains_ref[layer] = gain[layer : layer + 1, :] * (0.5 * HID**0.5)
    gains_ref[LAYERS] = dec_gain[...] * HID**0.5
    rows = [dec[...].astype(F32)[c : c + 1] for c in range(CHAN)]
    for x in range(BLOCK):
        part = jnp.concatenate(spread(rows, x), axis=0).astype(BF16)
        dec_out_ref[x // 2, :, (x % 2) * HID : (x % 2 + 1) * HID] = part
    copies[-1].wait()


def run_prepare(plan, rate_values, *arrays):
    vmem = pl.BlockSpec(memory_space=pltpu.VMEM)
    smem = pl.BlockSpec(memory_space=pltpu.SMEM)
    shapes = (
        ((FEATURES * BLOCK, BLOCK * HID), BF16),
        ((FEATURES * BLOCK, BLOCK * HID), BF16),
        ((LAYERS, HID, HID), BF16),
        ((LAYERS, 2 * HID, HID), BF16),
        ((LAYERS, 1, HID), F32),
        ((LAYERS + 1, 1, HID), F32),
        ((BLOCK // 2, CHAN * BLOCK, 2 * HID), BF16),
    )
    return pl.pallas_call(
        prepare,
        out_shape=tuple(jax.ShapeDtypeStruct(shape, dtype) for shape, dtype in shapes),
        in_specs=[smem] * 2 + [pl.BlockSpec(memory_space=pltpu.HBM)] * len(arrays),
        out_specs=(vmem,) * len(shapes),
        scratch_shapes=[pltpu.VMEM(array.shape, array.dtype) for array in arrays[:-1]]
        + [pltpu.SemaphoreType.DMA((len(arrays),))],
        compiler_params=pltpu.CompilerParams(vmem_limit_bytes=8 * 2**20),
        cost_estimate=pl.CostEstimate(flops=10**8, bytes_accessed=2**21, transcendentals=0),
        name="prepare",
    )(plan, rate_values, *arrays)


def exchange(value):
    count = lax.axis_size("space")
    first = [(i, i ^ 1) for i in range(count)]
    second = [(i, i + 1) for i in range(1, count - 1, 2)] + [(i + 1, i) for i in range(1, count - 1, 2)]
    return lax.ppermute(value, "space", first), lax.ppermute(value, "space", second)


def matvec(matrix, vector):
    return jnp.sum(matrix * vector[None], axis=1)


def matmat(left, right):
    return jnp.sum(left[:, :, None] * right[None], axis=1)


def per_device(
    prev_starts, plan, cell_type, coarse_matrix, rate_values, enc_weight, type_table, force_vector,
    norm_gain, self_weight, neigh_weight, out_weight, layer_bias, dec_gain, dec_weight,
):
    own = prev_starts[0]
    position = lax.axis_index("space")
    where = jnp.stack([position, lax.axis_size("space") - 1]).astype(jnp.int32)

    slabs = CHAN * NZ
    states = jnp.pad(own.reshape(slabs, BLOCK, NY), ((0, NZ), (0, 0), (0, 0)))
    types = jnp.pad(cell_type, ((slabs, 0), (0, 0), (0, 0))).astype(F32)
    slab = lax.broadcasted_iota(jnp.int32, states.shape, 0)
    outgoing = jnp.where(slab < slabs, states, types).astype(BF16).reshape(ROWS + NZ * BLOCK, NY)
    kinds = sides = exchange(outgoing)
    enc_first, enc_second, *weights = run_prepare(
        plan, rate_values, enc_weight, type_table, force_vector[None], norm_gain,
        out_weight, layer_bias, dec_gain[None], dec_weight, neigh_weight,
    )

    state = own
    for step_index in range(STEPS):
        state, outgoing = run_fine_step(
            where, state, *sides, cell_type, *kinds, (enc_first, enc_second)[step_index],
            self_weight, *weights,
        )
        if step_index + 1 < STEPS:
            sides = exchange(outgoing)

    window = lax.axis_index("tm")
    total = jnp.where(window == 0, state, state - matvec(coarse_matrix, own))
    corrected = total
    power, reach = coarse_matrix, coarse_matrix
    count = lax.axis_size("tm")
    distance = 1
    while distance < count:
        partners = [(i, i ^ SWAPS[distance]) for i in range(count)]
        came = lax.ppermute(total.astype(jnp.float16), "tm", partners).astype(F32)
        upper = (window // distance) % 2 == 1
        corrected = corrected + jnp.where(upper, matvec(reach, came), 0.0)
        if 2 * distance < count:
            lower_total = jnp.where(upper, came, total)
            upper_total = jnp.where(upper, total, came)
            total = upper_total + matvec(power, lower_total)
            reach = jnp.where(upper, matmat(power, reach), reach)
            power = matmat(power, power)
        distance *= 2
    return corrected[None]


def solution(mesh):
    return jax.shard_map(
        per_device,
        mesh=mesh,
        in_specs=(
            P("tm", None, None, "space", None),
            P("tm", None),
            P(None, "space", None),
            P(None, None, None, "space", None),
        )
        + (P(),) * 11,
        out_specs=P("tm", None, None, "space", None),
        check_vma=False,
    )
```

```python
import functools

import jax
import jax.numpy as jnp
from jax import lax
from jax.experimental import pallas as pl
from jax.experimental.pallas import tpu as pltpu
from jax.sharding import PartitionSpec as P

HID = 128
CHAN = 4
NZ = 4
TYPES = 3
RATES = 8
LAYERS = 6
STEPS = 2
NY = 128

EPS = 1e-05

GROUPS, GROUP = 8, 16
PADDED = (GROUPS + 2) * GROUP
BLOCK = 8
FRAME = 3 * BLOCK
SPARE = FRAME + 2
HELD = SPARE + 3
FEATURES = 2 * CHAN + 2 * TYPES
ROWS = CHAN * NZ * BLOCK

SWAPS = {1: 1, 2: 2, 4: 6, 8: 8, 16: 24}

F32, BF16 = jnp.float32, jnp.bfloat16


def dot(a, b, **kw):
    return jnp.dot(a, b, preferred_element_type=F32, **kw)


def dot_nt(a, b):
    return lax.dot_general(a, b, (((1,), (1,)), ((), ())), preferred_element_type=F32)


def twice(block):
    none = jnp.zeros_like(block)
    upper = jnp.concatenate([block, none], axis=1)
    return jnp.concatenate([upper, jnp.concatenate([none, block], axis=1)], axis=0)


def grouped(dtype):
    row = lax.broadcasted_iota(jnp.int32, (NY, NY), 0)
    cell = lax.broadcasted_iota(jnp.int32, (NY, NY), 1)
    return (cell == (row % GROUP) * GROUPS + row // GROUP).astype(dtype)


def fine_step(
    where_ref, own_ref, first_ref, second_ref, kind_ref, kind_first_ref, kind_second_ref,
    enc_ref, self_ref, neigh_ref, out_ref, bias_ref, gain_ref, dec_ref,
    state_ref, send_ref,
    hidden_ref, norm_ref, enter_ref,
):
    order = grouped(F32).astype(BF16)
    position = where_ref[0]
    last = where_ref[1]
    odd = position % 2 == 1
    at_left = position == 0
    at_right = position == last

    def strength(hidden):
        return jnp.sum(hidden * hidden, axis=-1, keepdims=True)

    def normalize(layer, hidden, target):
        normal = hidden * lax.rsqrt(strength(hidden) + HID * EPS) * gain_ref[layer]
        line = lax.broadcasted_iota(jnp.int32, (GROUP, HID), 0)
        before = jnp.where(line == 0, 0.0, pltpu.roll(normal[NY - GROUP :], 1, 0))
        after = jnp.where(line == GROUP - 1, 0.0, pltpu.roll(normal[:GROUP], GROUP - 1, 0))
        target[:GROUP, :] = before.astype(BF16)
        target[GROUP : GROUP + NY, :] = normal.astype(BF16)
        target[GROUP + NY :, :] = after.astype(BF16)

    @pl.when(at_left)
    def _():
        norm_ref[:, BLOCK - 1] = jnp.zeros((2, NZ, PADDED, HID), BF16)

    @pl.when(at_right)
    def _():
        norm_ref[:, 2 * BLOCK] = jnp.zeros((2, NZ, PADDED, HID), BF16)

    def encode(block, states, kinds, xs):
        turned = []
        for z in range(NZ):
            rows = [states[(c * NZ + z) * BLOCK : (c * NZ + z + 1) * BLOCK] for c in range(CHAN)]
            kind_row = kinds[z * BLOCK : (z + 1) * BLOCK]
            marks = [(kind_row == float(kind)).astype(F32) for kind in range(TYPES)]
            table = jnp.concatenate(rows + rows + marks + marks, axis=0).astype(BF16)
            turned.append(dot_nt(order, table).astype(BF16))
        turned = jnp.concatenate(turned, axis=0)
        for first in range(xs.start, xs.stop, 2):
            found = dot(turned, enc_ref[:, first * HID : (first + 2) * HID])
            for x in (first, first + 1):
                for z in range(NZ):
                    hidden = found[z * NY : (z + 1) * NY, (x - first) * HID : (x - first + 1) * HID]
                    hidden_ref[block * BLOCK + x, z] = hidden
                    normalize(0, hidden, norm_ref.at[0, block * BLOCK + x, z])

    encode(1, own_ref[...].reshape(ROWS, NY), kind_ref[...].reshape(NZ * BLOCK, NY).astype(F32), range(BLOCK))

    def neighbour(block, take_first, xs):
        states = jnp.where(take_first, first_ref[:ROWS, :], second_ref[:ROWS, :]).astype(F32)
        kinds = jnp.where(take_first, kind_first_ref[ROWS:, :], kind_second_ref[ROWS:, :]).astype(F32)
        encode(block, states, kinds, xs)

    @pl.when(jnp.logical_not(at_left))
    def _():
        neighbour(0, odd, range(BLOCK - LAYERS, BLOCK))

    @pl.when(jnp.logical_not(at_right))
    def _():
        neighbour(2, jnp.logical_not(odd), range(LAYERS))

    def rows_of(layer):
        reach = LAYERS - 1 - layer
        low = jnp.where(at_left, BLOCK, BLOCK - reach)
        high = jnp.where(at_right, 2 * BLOCK, 2 * BLOCK + reach)
        return low, high

    tiles = [(d, z) for d in range(2) for z in range(NZ)]

    def group(start):
        return slice(start * GROUP, (start + 1) * GROUP)

    def gather(layer, x):
        slot = layer % 2
        loaded = {}

        def read(dx, z, start, own=None):
            loaded_key = (dx, z, start, own)
            if loaded_key not in loaded:
                loaded[loaded_key] = norm_ref[slot, x + dx, z, group(start), :]
            return loaded[loaded_key]

        rows = []
        for d, z in tiles:
            for start in range(1, GROUPS + 1):
                key = (d, z)
                mid = read(d, z, start, key)
                along_x = read(d - 1, z, start, (key, 1)) + read(d + 1, z, start, (key, 1))
                along_y = read(d, z, start - 1, key) + read(d, z, start + 1, key)
                beside = [read(d, w, start, (key, 2)) for w in (z - 1, z + 1) if 0 <= w < NZ]
                along_z = functools.reduce(lambda a, b: a + b, beside)
                rows.append(jnp.concatenate([mid, along_x + along_y + along_z], axis=-1))
        return jnp.concatenate(rows, axis=0)

    def work(newest, second, third):
        if second is not None:
            half = enter_ref[...]
            message = half * jnp.tanh(half) + half
            leave = jnp.concatenate(
                [twice(out_ref[second[0], :HID]), twice(out_ref[second[0], HID:])], axis=0
            )
            moved = dot(jnp.concatenate([message, message], axis=-1), leave)
        if newest is not None:
            enter = jnp.concatenate([self_ref[newest[0]], neigh_ref[newest[0]]], axis=0)
            entered = dot(gather(*newest), enter)
            entered = (entered + bias_ref[newest[0]]).astype(BF16)
            for at, (d, z) in enumerate(tiles):
                enter_ref[z * NY : (z + 1) * NY, d * HID : (d + 1) * HID] = entered[at * NY : (at + 1) * NY]
        if third is not None:
            outside = jnp.logical_and(at_right, third[1] + 1 == 2 * BLOCK)
            slot = (third[0] + 1) % 2
            for d, z in tiles:
                row = third[1] if d == 0 else jnp.where(outside, SPARE, third[1] + 1)
                normalize(third[0] + 1, hidden_ref[third[1] + d, z], norm_ref.at[slot, row, z])
        if second is not None:
            for d, z in tiles:
                hidden_ref[second[1] + d, z] += moved[z * NY : (z + 1) * NY, d * HID : (d + 1) * HID]

    def after(pair):
        layer, x = pair
        ends = x + 2 >= rows_of(layer)[1]
        next_layer = jnp.where(ends, layer + 1, layer)
        next_x = jnp.where(ends, rows_of(layer + 1)[0], x + 2)
        done = next_layer >= LAYERS
        return (jnp.where(done, 0, next_layer), jnp.where(done, SPARE, next_x))

    def turn(_, pairs):
        newest, second, third = pairs
        work(newest, second, third)
        return after(newest), newest, second

    def count(layer):
        low, high = rows_of(layer)
        return (high - low + 1) // 2

    total = sum(count(layer) for layer in range(LAYERS))
    none = (jnp.int32(0), jnp.int32(SPARE))
    start = (jnp.int32(0), rows_of(0)[0])
    work(start, None, None)
    _, second, third = lax.fori_loop(0, total - 1, turn, (after(start), start, none))
    work(None, second, third)
    work(None, None, second)

    found = []
    for z in range(NZ):
        both = jnp.zeros((CHAN * BLOCK, NY), F32)
        for x in range(0, BLOCK, 2):
            pair = jnp.concatenate(
                [norm_ref[0, BLOCK + x + d, z, GROUP : GROUP + NY, :] for d in range(2)], axis=-1
            )
            both = both + dot_nt(dec_ref[x // 2], pair)
        found.append(both)
    change = dot(jnp.concatenate(found, axis=0), grouped(F32), precision=lax.Precision.HIGHEST)
    for c in range(CHAN):
        for z in range(NZ):
            at = (z * CHAN + c) * BLOCK
            state_ref[c, z] = own_ref[c, z] + change[at : at + BLOCK]
    send_ref[...] = state_ref[...].reshape(CHAN * NZ * BLOCK, NY).astype(BF16)


def run_fine_step(*args):
    vmem = pl.BlockSpec(memory_space=pltpu.VMEM)
    return pl.pallas_call(
        fine_step,
        out_shape=(
            jax.ShapeDtypeStruct((CHAN, NZ, BLOCK, NY), F32),
            jax.ShapeDtypeStruct((CHAN * NZ * BLOCK, NY), BF16),
        ),
        in_specs=[pl.BlockSpec(memory_space=pltpu.SMEM)] + [vmem] * 13,
        out_specs=(vmem, vmem),
        scratch_shapes=[
            pltpu.VMEM((HELD, NZ, NY, HID), F32),
            pltpu.VMEM((2, HELD, NZ, PADDED, HID), BF16),
            pltpu.VMEM((NZ * NY, 2 * HID), BF16),
        ],
        compiler_params=pltpu.CompilerParams(vmem_limit_bytes=26 * 2**20),
        cost_estimate=pl.CostEstimate(flops=10**10, bytes_accessed=2**21, transcendentals=10**7),
        name="fine_step",
    )(*args)


def centred(rows):
    return rows - jnp.mean(rows, axis=-1, keepdims=True)


def halves(value):
    high = value.astype(BF16)
    return high, (value - high.astype(F32)).astype(BF16)


def prepare(
    plan_ref, rate_ref,
    enc_hbm, type_hbm, force_hbm, gain_hbm, out_hbm, bias_hbm, dec_gain_hbm, dec_hbm, neigh_hbm,
    enc_first_ref, enc_second_ref, neigh_ref, leave_ref, bias_ref, gains_ref, dec_out_ref,
    enc, kind, force, gain, out, bias, dec_gain, dec, sems,
):
    sources = (enc_hbm, type_hbm, force_hbm, gain_hbm, out_hbm, bias_hbm, dec_gain_hbm, dec_hbm, neigh_hbm)
    targets = (enc, kind, force, gain, out, bias, dec_gain, dec, neigh_ref)
    copies = [pltpu.make_async_copy(a, b, sems.at[n]) for n, (a, b) in enumerate(zip(sources, targets))]
    for copy in copies:
        copy.start()
    for copy in copies[:-1]:
        copy.wait()

    line = lax.broadcasted_iota(jnp.int32, (BLOCK, HID), 0)

    def spread(rows, x):
        return [jnp.where(line == x, row, 0.0) for row in rows]

    weights = halves(centred(enc[...]))
    for step, enc_ref in enumerate((enc_first_ref, enc_second_ref)):
        rate = rate_ref[plan_ref[0, step]]
        push = rate * force[...]
        table = kind[...]
        kinds = halves(centred(jnp.concatenate([table[0:1], table[1:2] + push, table[2:3] - push], axis=0)))
        high, low = [half.astype(F32) for half in weights]
        rows = [part[c : c + 1] for part in (high, low) for c in range(CHAN)]
        rows += [part.astype(F32)[k : k + 1] for part in kinds for k in range(TYPES)]
        for x in range(BLOCK):
            enc_ref[:, x * HID : (x + 1) * HID] = jnp.concatenate(spread(rows, x), axis=0).astype(BF16)
    for layer in range(LAYERS):
        high, low = halves(centred(out[layer].astype(F32)))
        leave_ref[layer, :HID, :] = high
        leave_ref[layer, HID:, :] = low
        bias_ref[layer] = bias[layer : layer + 1, :] * 0.5
        gains_ref[layer] = gain[layer : layer + 1, :] * (0.5 * HID**0.5)
    gains_ref[LAYERS] = dec_gain[...] * HID**0.5
    rows = [dec[...].astype(F32)[c : c + 1] for c in range(CHAN)]
    for x in range(BLOCK):
        part = jnp.concatenate(spread(rows, x), axis=0).astype(BF16)
        dec_out_ref[x // 2, :, (x % 2) * HID : (x % 2 + 1) * HID] = part
    copies[-1].wait()


def run_prepare(plan, rate_values, *arrays):
    vmem = pl.BlockSpec(memory_space=pltpu.VMEM)
    smem = pl.BlockSpec(memory_space=pltpu.SMEM)
    shapes = (
        ((FEATURES * BLOCK, BLOCK * HID), BF16),
        ((FEATURES * BLOCK, BLOCK * HID), BF16),
        ((LAYERS, HID, HID), BF16),
        ((LAYERS, 2 * HID, HID), BF16),
        ((LAYERS, 1, HID), F32),
        ((LAYERS + 1, 1, HID), F32),
        ((BLOCK // 2, CHAN * BLOCK, 2 * HID), BF16),
    )
    return pl.pallas_call(
        prepare,
        out_shape=tuple(jax.ShapeDtypeStruct(shape, dtype) for shape, dtype in shapes),
        in_specs=[smem] * 2 + [pl.BlockSpec(memory_space=pltpu.HBM)] * len(arrays),
        out_specs=(vmem,) * len(shapes),
        scratch_shapes=[pltpu.VMEM(array.shape, array.dtype) for array in arrays[:-1]]
        + [pltpu.SemaphoreType.DMA((len(arrays),))],
        compiler_params=pltpu.CompilerParams(vmem_limit_bytes=8 * 2**20),
        cost_estimate=pl.CostEstimate(flops=10**8, bytes_accessed=2**21, transcendentals=0),
        name="prepare",
    )(plan, rate_values, *arrays)


def exchange(value):
    count = lax.axis_size("space")
    first = [(i, i ^ 1) for i in range(count)]
    second = [(i, i + 1) for i in range(1, count - 1, 2)] + [(i + 1, i) for i in range(1, count - 1, 2)]
    return lax.ppermute(value, "space", first), lax.ppermute(value, "space", second)


def matvec(matrix, vector):
    return jnp.sum(matrix * vector[None], axis=1)


def matmat(left, right):
    return jnp.sum(left[:, :, None] * right[None], axis=1)


def per_device(
    prev_starts, plan, cell_type, coarse_matrix, rate_values, enc_weight, type_table, force_vector,
    norm_gain, self_weight, neigh_weight, out_weight, layer_bias, dec_gain, dec_weight,
):
    own = prev_starts[0]
    position = lax.axis_index("space")
    where = jnp.stack([position, lax.axis_size("space") - 1]).astype(jnp.int32)

    slabs = CHAN * NZ
    states = jnp.pad(own.reshape(slabs, BLOCK, NY), ((0, NZ), (0, 0), (0, 0)))
    types = jnp.pad(cell_type, ((slabs, 0), (0, 0), (0, 0))).astype(F32)
    slab = lax.broadcasted_iota(jnp.int32, states.shape, 0)
    outgoing = jnp.where(slab < slabs, states, types).astype(BF16).reshape(ROWS + NZ * BLOCK, NY)
    kinds = sides = exchange(outgoing)
    enc_first, enc_second, *weights = run_prepare(
        plan, rate_values, enc_weight, type_table, force_vector[None], norm_gain,
        out_weight, layer_bias, dec_gain[None], dec_weight, neigh_weight,
    )

    state = own
    for step_index in range(STEPS):
        state, outgoing = run_fine_step(
            where, state, *sides, cell_type, *kinds, (enc_first, enc_second)[step_index],
            self_weight, *weights,
        )
        if step_index + 1 < STEPS:
            sides = exchange(outgoing)

    window = lax.axis_index("tm")
    total = jnp.where(window == 0, state, state - matvec(coarse_matrix, own))
    corrected = total
    power, reach = coarse_matrix, coarse_matrix
    count = lax.axis_size("tm")
    distance = 1
    while distance < count:
        partners = [(i, i ^ SWAPS[distance]) for i in range(count)]
        came = lax.ppermute(total.astype(jnp.float16), "tm", partners).astype(F32)
        upper = (window // distance) % 2 == 1
        corrected = corrected + jnp.where(upper, matvec(reach, came), 0.0)
        if 2 * distance < count:
            lower_total = jnp.where(upper, came, total)
            upper_total = jnp.where(upper, total, came)
            total = upper_total + matvec(power, lower_total)
            reach = jnp.where(upper, matmat(power, reach), reach)
            power = matmat(power, power)
        distance *= 2
    return corrected[None]


def solution(mesh):
    return jax.shard_map(
        per_device,
        mesh=mesh,
        in_specs=(
            P("tm", None, None, "space", None),
            P("tm", None),
            P(None, "space", None),
            P(None, None, None, "space", None),
        )
        + (P(),) * 11,
        out_specs=P("tm", None, None, "space", None),
        check_vma=False,
    )
```
